32 devices in a mesh: group: 4 (over z), sub: 8 (over y, x, core).
Axes of the slice: x: 2, y: 2, z: 4, core: 2. Of those that a mesh axis runs over, the one named last changes fastest.
Arguments:
- adjoint: float32 [4, 256, 65536], P(None, None, ('group', 'sub')), may hold values from -6 to 6
- velocity: bfloat16 [3, 256, 65536], P(None, None, ('group', 'sub')), may hold values from -6 to 6
- face_speed: bfloat16 [216, 65536], P(None, ('group', 'sub')), may hold values from -6 to 6
- derivatives: bfloat16 [768, 256], replicated, may hold values from -0.375 to 0.375
- lift_operator: bfloat16 [256, 216], replicated, may hold values from -1 to 1
- emission_profile: bfloat16 [256, 32], replicated, may hold values from -0.046875 to 0.046875
- neighbours: int32 [6, 65536], P(None, ('group', 'sub')), may hold values from 0 to 2815, as said below
- sub_sends: int32 [4, 16384], P(None, ('group', 'sub')), may hold values from 0 to 2047, as said below
- group_sends: int32 [2, 8192], P(None, ('group', 'sub')), may hold values from 0 to 2047, as said below
- element_tile: int32 [65536], P(('group', 'sub')), may hold values from 0 to 1023
- tile_slot: int32 [1024], replicated, may hold values from 0 to 1023, as said below
Outputs:
- adjoint_next: float32 [4, 256, 65536], P(None, None, ('group', 'sub'))
- emission_grad: float32 [1024, 128], P(('group', 'sub'))
The draws below stay inside these ranges and needn't reach their ends.
Inputs may be any that keep to these rules, and one draw needn't show every extreme that they name: `neighbours`: faces pair up symmetrically: face 2a + 1 of an element meets face 2a of exactly one element. Positions below 2048 name an element of the same partition; positions 2048 + r * 64 + j name slot j from partition r of the group, and are used only for faces 0 to 3; positions from 2560 on name the adjacent group's slots and are used only for faces 4 and 5. `sub_sends`: column (p * 8 + r) * 64 + j is partition p's slot j for partition r of its group. Between two distinct partitions of a group the same number of face pairs, 8 to 64, crosses in each of faces 0 and 1 and of faces 2 and 3, filling slots 0 onwards; in every group some pair has 64. Unused slots, and a partition's slots for itself, name element 0 and are read by nobody. `group_sends`: column p * 256 + j is partition p's slot j. Partitions of the same index q in adjacent groups share 256 // 2 to 256 face pairs, the same number for every group, filling slots 0 onwards; some q has 256. Unused slots name element 0 and are read by nobody. `tile_slot`: A permutation of the tiles onto the rows.
All inputs are finite; a program needn't handle non-finite values.
Results may differ from the reference program's by a relative error of at most 0.0032.
Values may be sent and summed in bfloat16 or wider, within the bound.
A program may use at most 192 MiB of HBM per device.

```python
import jax
import jax.numpy as jnp
import numpy as np
from jax import lax

ORDER = 5
NODES = 256
FACE = 36
TRACER_KINDS = 4
EMIT_HEIGHTS = 32
PART_ELEMENTS = 2048
CAP = 64
VCAP = 256
GROUPS = 4
SUBPARTS = 8
ELEMS = 65536
TILES = 1024
GROUP_TILES = 256


def mesh_lists(key):
    device_count = GROUPS * SUBPARTS
    block_len = PART_ELEMENTS // SUBPARTS
    low_count = max(1, CAP // 4)
    vertical_low = max(1, VCAP // 2)
    key_counts, key_first, key_second, key_vertical, key_vpick, key_shuffle = jax.random.split(key, 6)
    counts_raw = jax.random.randint(key_counts, (2, GROUPS, SUBPARTS, SUBPARTS), low_count, CAP + 1)
    row_ids = jnp.arange(SUBPARTS)[:, None]
    col_ids = jnp.arange(SUBPARTS)[None, :]
    pair_counts = jnp.where(row_ids < col_ids, counts_raw, jnp.swapaxes(counts_raw, 2, 3))
    first_pick = jax.random.randint(key_first, (2, GROUPS, 1, 1), 0, SUBPARTS)
    second_pick = (first_pick + jax.random.randint(key_second, (2, GROUPS, 1, 1), 1, SUBPARTS)) % SUBPARTS
    forced = (row_ids == first_pick) & (col_ids == second_pick) | (row_ids == second_pick) & (col_ids == first_pick)
    pair_counts = jnp.where(forced, CAP, pair_counts)
    pair_counts = jnp.where(row_ids == col_ids, 0, pair_counts)
    vertical_counts = jax.random.randint(key_vertical, (SUBPARTS,), vertical_low, VCAP + 1)
    vertical_pick = jax.random.randint(key_vpick, (), 0, SUBPARTS)
    vertical_counts = jnp.where(jnp.arange(SUBPARTS) == vertical_pick, VCAP, vertical_counts)

    def shuffled(subkey):
        return jax.random.permutation(subkey, PART_ELEMENTS).astype(jnp.int32)
    relabels = jax.vmap(shuffled)(jax.random.split(key_shuffle, device_count * 3)).reshape(device_count, 3, PART_ELEMENTS)

    def per_device(group_id, sub_id, relabel_all):
        structural = jnp.arange(PART_ELEMENTS, dtype=jnp.int32)
        offset_in = structural % block_len
        block_ids = structural // block_len
        slot_ids = jnp.arange(CAP, dtype=jnp.int32)
        vertical_slots = jnp.arange(VCAP, dtype=jnp.int32)
        peer_ids = jnp.arange(SUBPARTS, dtype=jnp.int32)[:, None]
        position_rows = []
        send_rows = []
        for axis_id in range(2):
            relabel = relabel_all[axis_id]
            peer_counts = pair_counts[axis_id, group_id, sub_id]
            crossing = peer_counts[block_ids]
            forward_local = relabel[block_ids * block_len + (offset_in + 1) % block_len]
            forward = jnp.where(offset_in < crossing, PART_ELEMENTS + block_ids * CAP + offset_in, forward_local)
            behind_local = relabel[block_ids * block_len + (offset_in - 1) % block_len]
            behind_remote = (offset_in >= 1) & (offset_in <= crossing)
            behind = jnp.where(behind_remote, PART_ELEMENTS + block_ids * CAP + offset_in - 1, behind_local)
            position_rows.append(jnp.zeros(PART_ELEMENTS, jnp.int32).at[relabel].set(behind))
            position_rows.append(jnp.zeros(PART_ELEMENTS, jnp.int32).at[relabel].set(forward))
            valid = slot_ids[None, :] < peer_counts[:, None]
            minus_elem = relabel[peer_ids * block_len + jnp.minimum(slot_ids[None, :] + 1, block_len - 1)]
            plus_elem = relabel[peer_ids * block_len + slot_ids[None, :]]
            send_rows.append(jnp.where(valid, minus_elem, 0).reshape(-1))
            send_rows.append(jnp.where(valid, plus_elem, 0).reshape(-1))
        relabel = relabel_all[2]
        vertical_reach = vertical_counts[sub_id]
        group_base = PART_ELEMENTS + SUBPARTS * CAP
        forward = jnp.where(structural < vertical_reach, group_base + structural, relabel[(structural + 1) % PART_ELEMENTS])
        behind_remote = (structural >= 1) & (structural <= vertical_reach)
        behind = jnp.where(behind_remote, group_base + structural - 1, relabel[(structural - 1) % PART_ELEMENTS])
        position_rows.append(jnp.zeros(PART_ELEMENTS, jnp.int32).at[relabel].set(behind))
        position_rows.append(jnp.zeros(PART_ELEMENTS, jnp.int32).at[relabel].set(forward))
        down_list = jnp.where(vertical_slots < vertical_reach, relabel[jnp.minimum(vertical_slots + 1, PART_ELEMENTS - 1)], 0)
        up_list = jnp.where(vertical_slots < vertical_reach, relabel[vertical_slots], 0)
        return (jnp.stack(position_rows), jnp.stack(send_rows), jnp.stack([down_list, up_list]))
    device_ids = jnp.arange(device_count, dtype=jnp.int32)
    positions, sends, vertical = jax.vmap(per_device)(device_ids // SUBPARTS, device_ids % SUBPARTS, relabels)
    positions = jnp.transpose(positions, (1, 0, 2)).reshape(6, device_count * PART_ELEMENTS)
    sends = jnp.transpose(sends, (1, 0, 2)).reshape(4, device_count * SUBPARTS * CAP)
    vertical = jnp.transpose(vertical, (1, 0, 2)).reshape(2, device_count * VCAP)
    return (positions.astype(jnp.int32), sends.astype(jnp.int32), vertical.astype(jnp.int32))


def draw_neighbours(key, part):
    return mesh_lists(jax.random.fold_in(key, 11))[0]


def draw_sub_sends(key, part):
    return mesh_lists(jax.random.fold_in(key, 11))[1]


def draw_group_sends(key, part):
    return mesh_lists(jax.random.fold_in(key, 11))[2]


def draw_element_tile(key, part):
    return jax.random.randint(key, (ELEMS,), 0, TILES).astype(jnp.int32)


def draw_tile_slot(key, part):

    def shuffled(subkey):
        return jax.random.permutation(subkey, GROUP_TILES).astype(jnp.int32)
    shuffles = jax.vmap(shuffled)(jax.random.split(key, GROUPS))
    bases = jnp.arange(GROUPS, dtype=jnp.int32)[:, None] * GROUP_TILES
    return (shuffles + bases).reshape(-1).astype(jnp.int32)


def levels(stream_key, extent, pieces, low, largest):
    factor_of, own = 1.0, jax.random.fold_in(stream_key, 6)
    for axis_at, blocks in pieces:
        heights = jnp.exp(jax.random.uniform(jax.random.fold_in(own, axis_at), (blocks,), jnp.float32, low / len(pieces), largest / len(pieces)))
        factor_of = factor_of * jnp.repeat(heights, extent[axis_at] // blocks).reshape([-1 if axis == axis_at else 1 for axis in range(len(extent))])
    return factor_of


def bell_draw(own_key, dims, deviation, limit, cuts=(), kind=jnp.bfloat16):
    loudness = levels(own_key, dims, cuts, -0.22, 0.18) if cuts else 1.0
    result = jax.random.normal(own_key, dims, jnp.float32) * deviation * loudness
    return jnp.minimum(jnp.maximum(result, -limit), limit).astype(kind)


def setup_inputs(seed: int = 0) -> dict:
    splits = jax.random.split(jax.random.key(seed), 12)
    adjoint = bell_draw(splits[0], (TRACER_KINDS, NODES, ELEMS), 1.0, 6.0, ((2, 32),), jnp.float32)
    velocity = bell_draw(splits[1], (3, NODES, ELEMS), 1.0, 6.0, ((2, 32),))
    face_speed = bell_draw(splits[2], (6 * FACE, ELEMS), 1.0, 6.0, ((1, 32),))
    derivatives = bell_draw(splits[3], (3 * NODES, NODES), NODES ** -0.5, 0.375)
    lift_operator = bell_draw(splits[4], (NODES, 6 * FACE), FACE ** -0.5, 1.0)
    emission_profile = bell_draw(splits[5], (NODES, EMIT_HEIGHTS), (NODES * PART_ELEMENTS * SUBPARTS // GROUP_TILES) ** -0.5, 0.046875)
    neighbours = draw_neighbours(jax.random.fold_in(splits[11], 71), 0)
    sub_sends = draw_sub_sends(jax.random.fold_in(splits[11], 71), 0)
    group_sends = draw_group_sends(jax.random.fold_in(splits[11], 71), 0)
    element_tile = draw_element_tile(jax.random.fold_in(splits[11], 71), 0)
    tile_slot = draw_tile_slot(jax.random.fold_in(splits[11], 71), 0)
    return {"adjoint": adjoint, "velocity": velocity, "face_speed": face_speed, "derivatives": derivatives, "lift_operator": lift_operator, "emission_profile": emission_profile, "neighbours": neighbours, "sub_sends": sub_sends, "group_sends": group_sends, "element_tile": element_tile, "tile_slot": tile_slot}


SECTION = 0.125


def face_table(order):
    edge_nodes = order + 1
    coords_a, coords_b = np.meshgrid(np.arange(edge_nodes), np.arange(edge_nodes), indexing="ij")
    coords_a = coords_a.reshape(-1)
    coords_b = coords_b.reshape(-1)
    face_rows = []
    for axis_id in range(3):
        for level_id in (0, edge_nodes - 1):
            fixed_col = coords_a * 0 + level_id
            if axis_id == 0:
                triple = (fixed_col, coords_a, coords_b)
            elif axis_id == 1:
                triple = (coords_a, fixed_col, coords_b)
            else:
                triple = (coords_a, coords_b, fixed_col)
            face_rows.append((triple[0] * edge_nodes + triple[1]) * edge_nodes + triple[2])
    return np.stack(face_rows).astype(np.int32)


def reference(adjoint, velocity, face_speed, derivatives, lift_operator, emission_profile, neighbours, sub_sends, group_sends, element_tile, tile_slot):
    face_rows = jnp.asarray(face_table(ORDER))
    device_count = GROUPS * SUBPARTS
    adjoint_lowered = lax.optimization_barrier(adjoint.astype(jnp.bfloat16))

    def columns(array, device_id, length):
        return lax.dynamic_slice_in_dim(array, device_id * length, length, array.ndim - 1)

    def build_sends(device_id):
        traces = columns(adjoint_lowered, device_id, PART_ELEMENTS)[:, face_rows, :]
        sub_list = columns(sub_sends, device_id, SUBPARTS * CAP)
        group_list = columns(group_sends, device_id, VCAP)
        sub_out = jnp.stack([jnp.take(traces[:, face_id], sub_list[face_id], axis=2) for face_id in range(4)])
        group_out = jnp.stack([jnp.take(traces[:, 4], group_list[0], axis=2), jnp.take(traces[:, 5], group_list[1], axis=2)])
        return sub_out, group_out

    sub_bufs, group_bufs = lax.map(build_sends, jnp.arange(device_count, dtype=jnp.int32))
    derivative_broad = derivatives.astype(jnp.float32)
    lift_broad = lift_operator.astype(jnp.float32)
    profile_broad = emission_profile.astype(jnp.float32)
    empty_sub = jnp.zeros((TRACER_KINDS, FACE, SUBPARTS * CAP), jnp.bfloat16)
    empty_group = jnp.zeros((TRACER_KINDS, FACE, VCAP), jnp.bfloat16)

    def one_device(running_total, device_id):
        group_id = device_id // SUBPARTS
        sub_id = device_id % SUBPARTS
        peer_bufs = lax.dynamic_slice_in_dim(sub_bufs, group_id * SUBPARTS, SUBPARTS, 0)
        for_me = lax.dynamic_slice_in_dim(peer_bufs, sub_id * CAP, CAP, 4)
        received = jnp.transpose(for_me, (1, 2, 3, 0, 4)).reshape(4, TRACER_KINDS, FACE, SUBPARTS * CAP)
        below_id = ((group_id + GROUPS - 1) % GROUPS) * SUBPARTS + sub_id
        above_id = ((group_id + 1) % GROUPS) * SUBPARTS + sub_id
        from_below = group_bufs[below_id, 1]
        from_above = group_bufs[above_id, 0]
        local_lowered = columns(adjoint_lowered, device_id, PART_ELEMENTS)
        traces = local_lowered[:, face_rows, :]
        nbr_dev = columns(neighbours, device_id, PART_ELEMENTS)
        outside_list = []
        for face_id in range(6):
            trace_id = face_id ^ 1
            sub_part = received[trace_id] if trace_id < 4 else empty_sub
            if trace_id == 5:
                group_part = from_below
            elif trace_id == 4:
                group_part = from_above
            else:
                group_part = empty_group
            pool_rows = jnp.concatenate([traces[:, trace_id], sub_part, group_part], axis=2)
            outside_list.append(jnp.take(pool_rows, nbr_dev[face_id], axis=2))
        outside = jnp.stack(outside_list, axis=1)
        upwind = jnp.maximum(columns(face_speed, device_id, PART_ELEMENTS).astype(jnp.float32), 0.0).reshape(6, FACE, PART_ELEMENTS)
        face_flux_values = (upwind * (outside.astype(jnp.float32) - traces.astype(jnp.float32))).astype(jnp.bfloat16)
        face_flux_values = lax.optimization_barrier(face_flux_values).reshape(TRACER_KINDS, 6 * FACE, PART_ELEMENTS)
        gradient_terms = jnp.einsum("hv,avr->ahr", derivative_broad, local_lowered.astype(jnp.float32))
        vel_dev = columns(velocity, device_id, PART_ELEMENTS).astype(jnp.float32)
        volume = vel_dev[0] * gradient_terms[:, :NODES] + vel_dev[1] * gradient_terms[:, NODES:2 * NODES] + vel_dev[2] * gradient_terms[:, 2 * NODES:]
        lifted_values = jnp.einsum("dq,wqx->wdx", lift_broad, face_flux_values.astype(jnp.float32))
        adjoint_next = columns(adjoint, device_id, PART_ELEMENTS) + SECTION * (volume + lifted_values)
        next_lowered = lax.optimization_barrier(adjoint_next.astype(jnp.bfloat16)).astype(jnp.float32)
        contribution = jnp.einsum("qvx,vj->xqj", next_lowered, profile_broad).reshape(PART_ELEMENTS, TRACER_KINDS * EMIT_HEIGHTS)
        tile_rows = jnp.take(tile_slot, columns(element_tile, device_id, PART_ELEMENTS))
        running_total = running_total + jax.ops.segment_sum(contribution, tile_rows, num_segments=TILES)
        return running_total, adjoint_next

    zero_total = jnp.zeros((TILES, TRACER_KINDS * EMIT_HEIGHTS), jnp.float32)
    totals, stacked = lax.scan(one_device, zero_total, jnp.arange(device_count, dtype=jnp.int32))
    adjoint_next = jnp.transpose(stacked, (1, 2, 0, 3)).reshape(TRACER_KINDS, NODES, device_count * PART_ELEMENTS)
    return adjoint_next, totals
```

```python
import functools

import jax
import jax.numpy as jnp
import numpy as np
from jax import lax
from jax.experimental import pallas as pl
from jax.experimental.pallas import tpu as pltpu
from jax.sharding import PartitionSpec as P

ORDER = 5
SECTION = 0.125
FACES = 6
SPAN = 256
MESH = pl.DeviceIdType.MESH
F32, BF16 = jnp.float32, jnp.bfloat16


def face_table(order):
    edge = order + 1
    a, b = np.meshgrid(np.arange(edge), np.arange(edge), indexing="ij")
    a, b = a.reshape(-1), b.reshape(-1)
    rows = []
    for axis_id in range(3):
        for level in (0, edge - 1):
            fixed = a * 0 + level
            i, j, l = [(fixed, a, b), (a, fixed, b), (a, b, fixed)][axis_id]
            rows.append((i * edge + j) * edge + l)
    return np.stack(rows).astype(np.int32)


def padded_nodes(face_nodes):
    return -(-face_nodes // 8) * 8


def select_matrix(node_count):
    table = face_table(ORDER)
    pad = padded_nodes(table.shape[1])
    out = np.zeros((FACES * pad, node_count), np.float32)
    for f in range(FACES):
        for k, n in enumerate(table[f]):
            out[f * pad + k, n] = 1
    return out


def spread_matrix(face_nodes):
    pad = padded_nodes(face_nodes)
    out = np.zeros((FACES * pad, FACES * face_nodes), np.float32)
    for f in range(FACES):
        for k in range(face_nodes):
            out[f * pad + k, f * face_nodes + k] = 1
    return out


def dot(a, b):
    return jnp.dot(a, b, preferred_element_type=F32)


def dot_nt(a, b):
    return lax.dot_general(a, b, (((1,), (1,)), ((), ())), preferred_element_type=F32)


def one_hot_rows(index, rows):
    ids = lax.broadcasted_iota(jnp.int32, (rows, index.shape[1]), 0)
    return jnp.where(ids == index, 1.0, 0.0).astype(BF16)


def columns_of(stack, position, first, count, block):
    picked = dot(stack, one_hot_rows(position & (SPAN - 1), SPAN))
    tile = position >> (SPAN.bit_length() - 1)
    out = jnp.zeros((block, position.shape[1]), F32)
    for t in range(count):
        out = jnp.where(tile == first + t, picked[t * block : (t + 1) * block], out)
    return out


def flux_kernel(
    n_group, n_sub, cap,
    adjoint, speed, neighbours, sub_sends, group_sends, select, spread,
    flux,
    field, table, local, send_sub, recv_sub, send_group, recv_group, far_sub,
    field_sem, sub_send_sem, sub_recv_sem, group_send_sem, group_recv_sem,
):
    tiles, species = field.shape[0], field.shape[1]
    pad = select.shape[0] // FACES
    block = species * pad
    elements = tiles * SPAN
    g, q = lax.axis_index("group"), lax.axis_index("sub")
    above = (lax.rem(g + 1, n_group), q)
    below = (lax.rem(g + n_group - 1, n_group), q)

    def field_copy(i):
        cols = pl.ds(pl.multiple_of(i * SPAN, SPAN), SPAN)
        return pltpu.make_async_copy(adjoint.at[:, :, cols], field.at[i], field_sem.at[i])

    for i in range(tiles):
        field_copy(i).start()

    barrier = pltpu.get_barrier_semaphore()
    peers = [(g, lax.rem(q + d, n_sub)) for d in range(1, n_sub)] + [above, below]
    for peer in peers:
        pl.semaphore_signal(barrier, inc=1, device_id=peer, device_id_type=MESH)

    def trace_tile(i, carry):
        field_copy(i).wait()
        parts = [dot(select[...], field[i, s].astype(BF16)) for s in range(species)]
        rows = pl.ds(pl.multiple_of(i * block, block), block)
        for f in range(FACES):
            one = jnp.concatenate([p[f * pad : (f + 1) * pad] for p in parts], axis=0)
            table[f, rows, :] = one.astype(BF16)
        return carry

    lax.fori_loop(0, tiles, trace_tile, 0)

    low_half = lax.broadcasted_iota(jnp.int32, (block, 2 * cap), 1) < cap
    for axis_id in range(2):
        for c in range(n_sub * cap // SPAN):
            cols = slice(c * SPAN, (c + 1) * SPAN)
            minus, plus = [
                columns_of(table[f], sub_sends[f : f + 1, cols], 0, tiles, block)
                for f in (2 * axis_id, 2 * axis_id + 1)
            ]
            for m in range(SPAN // (2 * cap)):
                part = slice(m * 2 * cap, (m + 1) * 2 * cap)
                a, b = minus[:, part], plus[:, part]
                r = c * (SPAN // cap) + 2 * m
                send_sub[r, axis_id] = jnp.where(low_half, a, pltpu.roll(b, cap, 1)).astype(BF16)
                send_sub[r + 1, axis_id] = jnp.where(low_half, pltpu.roll(a, cap, 1), b).astype(BF16)
    pl.semaphore_wait(barrier, len(peers))
    copies = []
    for d in range(1, n_sub):
        peer = lax.rem(q + d, n_sub)
        copies.append(
            pltpu.make_async_remote_copy(
                src_ref=send_sub.at[peer], dst_ref=recv_sub.at[q],
                send_sem=sub_send_sem.at[d], recv_sem=sub_recv_sem.at[d],
                device_id=(g, peer), device_id_type=MESH,
            )
        )
        copies[-1].start()
    span_group = send_group.shape[2]
    for k, target in ((0, below), (1, above)):
        for c in range(span_group // SPAN):
            cols = slice(c * SPAN, (c + 1) * SPAN)
            got = columns_of(table[4 + k], group_sends[k : k + 1, cols], 0, tiles, block)
            send_group[k, :, cols] = got.astype(BF16)
        copies.append(
            pltpu.make_async_remote_copy(
                src_ref=send_group.at[k], dst_ref=recv_group.at[k],
                send_sem=group_send_sem.at[k], recv_sem=group_recv_sem.at[k],
                device_id=target, device_id_type=MESH,
            )
        )
        copies[-1].start()
    recv_sub[q] = jnp.zeros(recv_sub.shape[1:], BF16)

    def local_tile(i, carry):
        cols = pl.ds(pl.multiple_of(i * SPAN, SPAN), SPAN)
        for f in range(FACES):
            got = columns_of(table[f ^ 1], neighbours[f : f + 1, cols], 0, tiles, block)
            local[f, :, cols] = got.astype(BF16)
        return carry

    lax.fori_loop(0, tiles, local_tile, 0)

    for copy in copies:
        copy.wait()
    far_tiles = n_sub * cap // SPAN
    for t in range(4):
        for r in range(0, n_sub, 2):
            a = recv_sub[r, t // 2].astype(F32)
            b = recv_sub[r + 1, t // 2].astype(F32)
            if t % 2 == 0:
                both = jnp.where(low_half, a, pltpu.roll(b, cap, 1))
            else:
                both = jnp.where(low_half, pltpu.roll(a, cap, 1), b)
            lane = r * cap
            far_sub[t, (lane // SPAN) * block : (lane // SPAN + 1) * block,
                    lane % SPAN : lane % SPAN + 2 * cap] = both.astype(BF16)

    def flux_tile(i, carry):
        cols = pl.ds(pl.multiple_of(i * SPAN, SPAN), SPAN)
        rows = pl.ds(pl.multiple_of(i * block, block), block)
        upwind = jnp.maximum(dot(spread[...], speed[:, cols]), 0.0)
        parts = []
        for f in range(FACES):
            t = f ^ 1
            position = neighbours[f : f + 1, cols]
            if t < 4:
                far = columns_of(far_sub[t], position, tiles, far_tiles, block)
            else:
                far = jnp.zeros((block, SPAN), F32)
                for c in range(span_group // SPAN):
                    got = recv_group[t - 4, :, c * SPAN : (c + 1) * SPAN]
                    far += columns_of(got, position, tiles + far_tiles + c, 1, block)
            outside = local[f, :, cols].astype(F32) + far
            wind = jnp.concatenate([upwind[f * pad : (f + 1) * pad]] * species, axis=0)
            parts.append(wind * (outside - table[f, rows, :].astype(F32)))
        for s in range(species):
            one = jnp.concatenate([p[s * pad : (s + 1) * pad] for p in parts], axis=0)
            flux[s, :, cols] = one.astype(BF16)
        return carry

    lax.fori_loop(0, tiles, flux_tile, 0)


def step_kernel(
    adjoint, velocity, flux, derivatives, lift, profile, spread, element_tile, tile_slot,
    adjoint_next, partial, lift_wide,
):
    species, nodes, span = adjoint.shape
    tile_rows = partial.shape[0]

    @pl.when(pl.program_id(0) == 0)
    def _():
        lift_wide[...] = dot_nt(lift[...], spread[...]).astype(BF16)
        partial[...] = jnp.zeros_like(partial)

    tile = element_tile[...]
    width = tile_slot.shape[1]
    slots = tile_slot[...]
    high = dot((slots >> 8).astype(F32).astype(BF16), one_hot_rows(lax.rem(tile, width), width))
    low = dot((slots & 255).astype(F32).astype(BF16), one_hot_rows(lax.rem(tile, width), width))
    picked = (high * 256.0 + low)
    which = lax.broadcasted_iota(jnp.int32, picked.shape, 0) == lax.div(tile, width)
    row = jnp.sum(jnp.where(which, picked, 0.0), axis=0, keepdims=True).astype(jnp.int32)

    contrib = []
    for s in range(species):
        field = adjoint[s]
        grads = dot(derivatives[...], field.astype(BF16))
        total = dot(lift_wide[...], flux[s])
        for d in range(3):
            total += velocity[d].astype(F32) * grads[d * nodes : (d + 1) * nodes]
        result = field + SECTION * total
        adjoint_next[s] = result
        contrib.append(lax.dot_general(
            profile[...], result.astype(BF16), (((0,), (0,)), ((), ())), preferred_element_type=F32))
    terms = jnp.concatenate(contrib, axis=0)
    first = terms.astype(BF16)
    second = (terms - first.astype(F32)).astype(BF16)
    both = jnp.concatenate([first, second], axis=0)
    sums = dot_nt(one_hot_rows(row, tile_rows), both)
    half = terms.shape[0]
    partial[...] += sums[:, :half] + sums[:, half:]


def sum_kernel(
    n_group, n_sub,
    partial, out,
    send, recv, mid, recv_mid,
    send_sem, recv_sem, mid_send_sem, mid_recv_sem,
):
    own = out.shape[0]
    g, q = lax.axis_index("group"), lax.axis_index("sub")
    barrier = pltpu.get_barrier_semaphore()
    peers = [(g, lax.rem(q + d, n_sub)) for d in range(1, n_sub)]
    peers += [(lax.rem(g + d, n_group), q) for d in range(1, n_group)]
    for peer in peers:
        pl.semaphore_signal(barrier, inc=1, device_id=peer, device_id_type=MESH)

    def rows_of(group, sub):
        return pl.ds(pl.multiple_of((group * n_sub + sub) * own, own), own)

    for d in range(1, n_sub):
        for k in range(n_group):
            send[d, k] = partial[rows_of(k, lax.rem(q + d, n_sub)), :].astype(BF16)
    pl.semaphore_wait(barrier, len(peers))
    copies = []
    for d in range(1, n_sub):
        copies.append(
            pltpu.make_async_remote_copy(
                src_ref=send.at[d], dst_ref=recv.at[d],
                send_sem=send_sem.at[d], recv_sem=recv_sem.at[d],
                device_id=(g, lax.rem(q + d, n_sub)), device_id_type=MESH,
            )
        )
        copies[-1].start()
    for k in range(n_group):
        mid[k] = partial[rows_of(k, q), :]
    for copy in copies:
        copy.wait()
    for k in range(n_group):
        total = mid[k]
        for d in range(1, n_sub):
            total += recv[d, k].astype(F32)
        mid[k] = total
    copies = []
    for d in range(1, n_group):
        other = lax.rem(g + d, n_group)
        copies.append(
            pltpu.make_async_remote_copy(
                src_ref=mid.at[other], dst_ref=recv_mid.at[d],
                send_sem=mid_send_sem.at[d], recv_sem=mid_recv_sem.at[d],
                device_id=(other, q), device_id_type=MESH,
            )
        )
        copies[-1].start()
    for copy in copies:
        copy.wait()
    total = mid[g]
    for d in range(1, n_group):
        total += recv_mid[d]
    out[...] = total


def on_device(
    n_group, n_sub,
    adjoint, velocity, face_speed, derivatives, lift_operator, emission_profile,
    neighbours, sub_sends, group_sends, element_tile, tile_slot,
):
    species, nodes, elements = adjoint.shape
    face_nodes = face_speed.shape[0] // FACES
    pad = padded_nodes(face_nodes)
    block = species * pad
    tiles = elements // SPAN
    cap = sub_sends.shape[1] // n_sub
    span_group = group_sends.shape[1]
    assert elements % SPAN == 0 and SPAN % (2 * cap) == 0 and 2 * cap == 128
    assert (n_sub * cap) % SPAN == 0 and span_group % SPAN == 0
    select = jnp.asarray(select_matrix(nodes), BF16)
    spread = jnp.asarray(spread_matrix(face_nodes), BF16)
    vmem = pl.BlockSpec(memory_space=pltpu.VMEM)
    dma = pltpu.SemaphoreType.DMA
    far_tiles = n_sub * cap // SPAN

    flux = pl.pallas_call(
        functools.partial(flux_kernel, n_group, n_sub, cap),
        out_shape=jax.ShapeDtypeStruct((species, FACES * pad, elements), BF16),
        in_specs=[pl.BlockSpec(memory_space=pl.ANY)] + [vmem] * 6,
        out_specs=vmem,
        scratch_shapes=[
            pltpu.VMEM((tiles, species, nodes, SPAN), F32),
            pltpu.VMEM((FACES, tiles * block, SPAN), BF16),
            pltpu.VMEM((FACES, block, elements), BF16),
            pltpu.VMEM((n_sub, 2, block, 2 * cap), BF16),
            pltpu.VMEM((n_sub, 2, block, 2 * cap), BF16),
            pltpu.VMEM((2, block, span_group), BF16),
            pltpu.VMEM((2, block, span_group), BF16),
            pltpu.VMEM((4, far_tiles * block, SPAN), BF16),
            dma((tiles,)), dma((n_sub,)), dma((n_sub,)), dma((2,)), dma((2,)),
        ],
        compiler_params=pltpu.CompilerParams(
            collective_id=0, has_side_effects=True, vmem_limit_bytes=56 * 2**20),
        name="flux",
    )(adjoint, face_speed, neighbours, sub_sends, group_sends, select, spread)

    tile_count = tile_slot.shape[0]
    heights = emission_profile.shape[1]
    whole = lambda shape: pl.BlockSpec(shape, lambda i: (0,) * len(shape))
    along = lambda *lead: pl.BlockSpec(lead + (SPAN,), lambda i: (0,) * len(lead) + (i,))
    slots = tile_slot.reshape(tile_count // 128, 128)
    adjoint_next, partial = pl.pallas_call(
        step_kernel,
        grid=(tiles,),
        out_shape=(
            jax.ShapeDtypeStruct(adjoint.shape, F32),
            jax.ShapeDtypeStruct((tile_count, species * heights), F32),
        ),
        in_specs=[
            along(species, nodes), along(velocity.shape[0], nodes), along(species, FACES * pad),
            whole(derivatives.shape), whole(lift_operator.shape), whole(emission_profile.shape),
            whole(spread.shape), along(1), whole(slots.shape),
        ],
        out_specs=(along(species, nodes), whole((tile_count, species * heights))),
        scratch_shapes=[pltpu.VMEM((nodes, FACES * pad), BF16)],
        compiler_params=pltpu.CompilerParams(vmem_limit_bytes=56 * 2**20),
        name="step",
    )(
        adjoint, velocity, flux, derivatives, lift_operator, emission_profile,
        spread, element_tile.reshape(1, elements), slots,
    )

    own = tile_count // (n_group * n_sub)
    width = species * heights
    emission_grad = pl.pallas_call(
        functools.partial(sum_kernel, n_group, n_sub),
        out_shape=jax.ShapeDtypeStruct((own, width), F32),
        in_specs=[vmem],
        out_specs=vmem,
        scratch_shapes=[
            pltpu.VMEM((n_sub, n_group, own, width), BF16),
            pltpu.VMEM((n_sub, n_group, own, width), BF16),
            pltpu.VMEM((n_group, own, width), F32),
            pltpu.VMEM((n_group, own, width), F32),
            dma((n_sub,)), dma((n_sub,)), dma((n_group,)), dma((n_group,)),
        ],
        compiler_params=pltpu.CompilerParams(
            collective_id=1, has_side_effects=True, vmem_limit_bytes=16 * 2**20),
        name="sum",
    )(partial)
    return adjoint_next, emission_grad


def solution(mesh):
    both = ("group", "sub")
    placed = (
        P(None, None, both), P(None, None, both), P(None, both), P(), P(), P(),
        P(None, both), P(None, both), P(None, both), P(both), P(),
    )
    return jax.shard_map(
        functools.partial(on_device, mesh.shape["group"], mesh.shape["sub"]),
        mesh=mesh,
        in_specs=placed,
        out_specs=(P(None, None, both), P(both, None)),
        check_vma=False,
    )
```

```python
import functools

import jax
import jax.numpy as jnp
import numpy as np
from jax import lax
from jax.experimental import pallas as pl
from jax.experimental.pallas import tpu as pltpu
from jax.sharding import PartitionSpec as P

ORDER = 5
SECTION = 0.125
FACES = 6
SPAN = 256
WIDE = 512
MESH = pl.DeviceIdType.MESH
F32, BF16 = jnp.float32, jnp.bfloat16


def face_table(order):
    edge = order + 1
    a, b = np.meshgrid(np.arange(edge), np.arange(edge), indexing="ij")
    a, b = a.reshape(-1), b.reshape(-1)
    rows = []
    for axis_id in range(3):
        for level in (0, edge - 1):
            fixed = a * 0 + level
            i, j, l = [(fixed, a, b), (a, fixed, b), (a, b, fixed)][axis_id]
            rows.append((i * edge + j) * edge + l)
    return np.stack(rows).astype(np.int32)


def padded_nodes(face_nodes):
    return -(-face_nodes // 8) * 8


def select_matrix(node_count):
    table = face_table(ORDER)
    pad = padded_nodes(table.shape[1])
    out = np.zeros((FACES * pad, node_count), np.float32)
    for f in range(FACES):
        for k, n in enumerate(table[f]):
            out[f * pad + k, n] = 1
    return out


def spread_matrix(face_nodes):
    pad = padded_nodes(face_nodes)
    out = np.zeros((FACES * pad, FACES * face_nodes), np.float32)
    for f in range(FACES):
        for k in range(face_nodes):
            out[f * pad + k, f * face_nodes + k] = 1
    return out


def dot(a, b):
    return jnp.dot(a, b, preferred_element_type=F32)


def dot_nt(a, b):
    return lax.dot_general(a, b, (((1,), (1,)), ((), ())), preferred_element_type=F32)


def one_hot_rows(index, rows):
    ids = lax.broadcasted_iota(jnp.int32, (rows, index.shape[1]), 0).astype(jnp.int16)
    return jnp.where(ids == index.astype(jnp.int16), jnp.ones((), BF16), jnp.zeros((), BF16))


def columns_of(stack, position, first, count, block):
    picked = dot(stack, one_hot_rows(position & (SPAN - 1), SPAN))
    tile = position >> (SPAN.bit_length() - 1)
    out = picked[:block]
    for t in range(1, count):
        out = jnp.where(tile == first + t, picked[t * block : (t + 1) * block], out)
    return out


def flux_kernel(
    n_group, n_sub, cap,
    adjoint, speed, neighbours, sub_sends, group_sends, select, spread,
    flux,
    field, table, local, send_sub, recv_sub, send_group, recv_group, far_sub,
    field_sem, sub_send_sem, sub_recv_sem, group_send_sem, group_recv_sem,
):
    tiles, species = field.shape[0], field.shape[1]
    pad = select.shape[0] // FACES
    block = species * pad
    elements = tiles * SPAN
    g, q = lax.axis_index("group"), lax.axis_index("sub")
    above = (lax.rem(g + 1, n_group), q)
    below = (lax.rem(g + n_group - 1, n_group), q)

    def field_copy(i):
        cols = pl.ds(pl.multiple_of(i * SPAN, SPAN), SPAN)
        return pltpu.make_async_copy(adjoint.at[:, :, cols], field.at[i], field_sem.at[i])

    for i in range(tiles):
        field_copy(i).start()

    barrier = pltpu.get_barrier_semaphore()
    peers = [(g, lax.rem(q + d, n_sub)) for d in range(1, n_sub)] + [above, below]
    for peer in peers:
        pl.semaphore_signal(barrier, inc=1, device_id=peer, device_id_type=MESH)

    def trace_tile(i, carry):
        for j in range(WIDE // SPAN):
            field_copy(i * (WIDE // SPAN) + j).wait()
        for j in range(WIDE // SPAN):
            tile = i * (WIDE // SPAN) + j
            parts = [dot(select[...], field[tile, s].astype(BF16)) for s in range(species)]
            rows = pl.ds(pl.multiple_of(tile * block, block), block)
            for f in range(FACES):
                one = jnp.concatenate([p[f * pad : (f + 1) * pad] for p in parts], axis=0)
                table[f, rows, :] = one.astype(BF16)
        return carry

    lax.fori_loop(0, tiles * SPAN // WIDE, trace_tile, 0)

    low_half = lax.broadcasted_iota(jnp.int32, (block, 2 * cap), 1) < cap
    for axis_id in range(2):
        for c in range(n_sub * cap // WIDE):
            cols = slice(c * WIDE, (c + 1) * WIDE)
            minus, plus = [
                columns_of(table[f], sub_sends[f : f + 1, cols], 0, tiles, block)
                for f in (2 * axis_id, 2 * axis_id + 1)
            ]
            for m in range(WIDE // (2 * cap)):
                part = slice(m * 2 * cap, (m + 1) * 2 * cap)
                a, b = minus[:, part], plus[:, part]
                r = c * (WIDE // cap) + 2 * m
                send_sub[r, axis_id] = jnp.where(low_half, a, pltpu.roll(b, cap, 1)).astype(BF16)
                send_sub[r + 1, axis_id] = jnp.where(low_half, pltpu.roll(a, cap, 1), b).astype(BF16)
    pl.semaphore_wait(barrier, len(peers))
    copies = []
    for d in range(1, n_sub):
        peer = lax.rem(q + d, n_sub)
        copies.append(
            pltpu.make_async_remote_copy(
                src_ref=send_sub.at[peer], dst_ref=recv_sub.at[q],
                send_sem=sub_send_sem.at[d], recv_sem=sub_recv_sem.at[d],
                device_id=(g, peer), device_id_type=MESH,
            )
        )
        copies[-1].start()
    span_group = send_group.shape[2]
    for k, target in ((0, below), (1, above)):
        for c in range(span_group // SPAN):
            cols = slice(c * SPAN, (c + 1) * SPAN)
            got = columns_of(table[4 + k], group_sends[k : k + 1, cols], 0, tiles, block)
            send_group[k, :, cols] = got.astype(BF16)
        copies.append(
            pltpu.make_async_remote_copy(
                src_ref=send_group.at[k], dst_ref=recv_group.at[k],
                send_sem=group_send_sem.at[k], recv_sem=group_recv_sem.at[k],
                device_id=target, device_id_type=MESH,
            )
        )
        copies[-1].start()
    recv_sub[q] = jnp.zeros(recv_sub.shape[1:], BF16)

    def local_tile(i, carry):
        cols = pl.ds(pl.multiple_of(i * WIDE, WIDE), WIDE)
        for f in range(FACES):
            got = columns_of(table[f ^ 1], neighbours[f : f + 1, cols], 0, tiles, block)
            local[f, :, cols] = got.astype(BF16)
        return carry

    lax.fori_loop(0, elements // WIDE, local_tile, 0)

    for copy in copies:
        copy.wait()
    far_tiles = n_sub * cap // SPAN
    for t in range(4):
        for r in range(0, n_sub, 2):
            a = recv_sub[r, t // 2].astype(F32)
            b = recv_sub[r + 1, t // 2].astype(F32)
            if t % 2 == 0:
                both = jnp.where(low_half, a, pltpu.roll(b, cap, 1))
            else:
                both = jnp.where(low_half, pltpu.roll(a, cap, 1), b)
            lane = r * cap
            far_sub[t, (lane // SPAN) * block : (lane // SPAN + 1) * block,
                    lane % SPAN : lane % SPAN + 2 * cap] = both.astype(BF16)

    def flux_tile(i, carry):
        cols = pl.ds(pl.multiple_of(i * WIDE, WIDE), WIDE)
        inside = WIDE // SPAN
        upwind = jnp.maximum(dot(spread[...], speed[:, cols]), 0.0)
        parts = []
        for f in range(FACES):
            t = f ^ 1
            position = neighbours[f : f + 1, cols]
            if t < 4:
                far = columns_of(far_sub[t], position, tiles, far_tiles, block)
            else:
                stack = jnp.concatenate([
                    recv_group[t - 4, :, c * SPAN : (c + 1) * SPAN]
                    for c in range(span_group // SPAN)
                ], axis=0)
                far = columns_of(stack, position, tiles + far_tiles, span_group // SPAN, block)
            outside = jnp.where(position >= elements, far, local[f, :, cols].astype(F32))
            wind = jnp.concatenate([upwind[f * pad : (f + 1) * pad]] * species, axis=0)
            here = jnp.concatenate([
                table[f, pl.ds(pl.multiple_of((i * inside + j) * block, block), block), :]
                for j in range(inside)
            ], axis=1)
            parts.append(wind * (outside - here.astype(F32)))
        for s in range(species):
            one = jnp.concatenate([p[s * pad : (s + 1) * pad] for p in parts], axis=0)
            flux[s, :, cols] = one.astype(BF16)
        return carry

    lax.fori_loop(0, elements // WIDE, flux_tile, 0)


def step_kernel(
    adjoint, velocity, flux, derivatives, lift, profile, spread, element_tile, tile_slot,
    adjoint_next, partial, lift_wide,
):
    species, nodes, span = adjoint.shape
    tile_rows = partial.shape[0]

    @pl.when(pl.program_id(0) == 0)
    def _():
        lift_wide[...] = dot(spread[...], lift[...]).T.astype(BF16)
        partial[...] = jnp.zeros_like(partial)

    tile = element_tile[...]
    width = tile_slot.shape[1]
    slots = tile_slot[...]
    high = dot((slots >> 8).astype(F32).astype(BF16), one_hot_rows(lax.rem(tile, width), width))
    low = dot((slots & 255).astype(F32).astype(BF16), one_hot_rows(lax.rem(tile, width), width))
    picked = (high * 256.0 + low)
    which = lax.broadcasted_iota(jnp.int32, picked.shape, 0) == lax.div(tile, width)
    row = jnp.sum(jnp.where(which, picked, 0.0), axis=0, keepdims=True).astype(jnp.int32)

    contrib = []
    wind = [velocity[d].astype(F32) for d in range(3)]
    for s in range(species):
        field = adjoint[s]
        grads = dot(derivatives[...], field.astype(BF16))
        total = dot(lift_wide[...], flux[s])
        for d in range(3):
            total += wind[d] * grads[d * nodes : (d + 1) * nodes]
        result = field + SECTION * total
        adjoint_next[s] = result
        contrib.append(dot(profile[...], result.astype(BF16)))
    terms = jnp.concatenate(contrib, axis=0)
    first = terms.astype(BF16)
    second = (terms - first.astype(F32)).astype(BF16)
    both = jnp.concatenate([first, second], axis=0)
    sums = dot_nt(one_hot_rows(row, tile_rows), both)
    half = terms.shape[0]
    partial[...] += sums[:, :half] + sums[:, half:]


def sum_kernel(
    n_group, n_sub,
    partial_hbm, out,
    partial, send, recv, mid, recv_mid,
    load_sem, send_sem, recv_sem, mid_send_sem, mid_recv_sem,
):
    load = pltpu.make_async_copy(partial_hbm, partial, load_sem)
    load.start()
    own = out.shape[0]
    g, q = lax.axis_index("group"), lax.axis_index("sub")
    barrier = pltpu.get_barrier_semaphore()
    peers = [(g, lax.rem(q + d, n_sub)) for d in range(1, n_sub)]
    peers += [(lax.rem(g + d, n_group), q) for d in range(1, n_group)]
    for peer in peers:
        pl.semaphore_signal(barrier, inc=1, device_id=peer, device_id_type=MESH)

    def rows_of(group, sub):
        return pl.ds(pl.multiple_of((group * n_sub + sub) * own, own), own)

    load.wait()
    for d in range(1, n_sub):
        for k in range(n_group):
            send[d, k] = partial[rows_of(k, lax.rem(q + d, n_sub)), :].astype(BF16)
    pl.semaphore_wait(barrier, len(peers))
    copies = []
    for d in range(1, n_sub):
        copies.append(
            pltpu.make_async_remote_copy(
                src_ref=send.at[d], dst_ref=recv.at[d],
                send_sem=send_sem.at[d], recv_sem=recv_sem.at[d],
                device_id=(g, lax.rem(q + d, n_sub)), device_id_type=MESH,
            )
        )
        copies[-1].start()
    for k in range(n_group):
        mid[k] = partial[rows_of(k, q), :]
    for copy in copies:
        copy.wait()
    for k in range(n_group):
        total = mid[k]
        for d in range(1, n_sub):
            total += recv[d, k].astype(F32)
        mid[k] = total
    copies = []
    for d in range(1, n_group):
        other = lax.rem(g + d, n_group)
        copies.append(
            pltpu.make_async_remote_copy(
                src_ref=mid.at[other], dst_ref=recv_mid.at[d],
                send_sem=mid_send_sem.at[d], recv_sem=mid_recv_sem.at[d],
                device_id=(other, q), device_id_type=MESH,
            )
        )
        copies[-1].start()
    for copy in copies:
        copy.wait()
    total = mid[g]
    for d in range(1, n_group):
        total += recv_mid[d]
    out[...] = total


def on_device(
    n_group, n_sub,
    adjoint, velocity, face_speed, derivatives, lift_operator, emission_profile,
    neighbours, sub_sends, group_sends, element_tile, tile_slot,
):
    species, nodes, elements = adjoint.shape
    face_nodes = face_speed.shape[0] // FACES
    pad = padded_nodes(face_nodes)
    block = species * pad
    tiles = elements // SPAN
    cap = sub_sends.shape[1] // n_sub
    span_group = group_sends.shape[1]
    assert elements % WIDE == 0 and n_sub * cap % WIDE == 0 and SPAN % (2 * cap) == 0 and 2 * cap == 128
    assert (n_sub * cap) % SPAN == 0 and span_group % SPAN == 0
    select = jnp.asarray(select_matrix(nodes), BF16)
    spread = jnp.asarray(spread_matrix(face_nodes), BF16)
    vmem = pl.BlockSpec(memory_space=pltpu.VMEM)
    dma = pltpu.SemaphoreType.DMA
    far_tiles = n_sub * cap // SPAN

    flux = pl.pallas_call(
        functools.partial(flux_kernel, n_group, n_sub, cap),
        out_shape=jax.ShapeDtypeStruct((species, FACES * pad, elements), BF16),
        in_specs=[pl.BlockSpec(memory_space=pl.ANY)] + [vmem] * 6,
        out_specs=vmem,
        scratch_shapes=[
            pltpu.VMEM((tiles, species, nodes, SPAN), F32),
            pltpu.VMEM((FACES, tiles * block, SPAN), BF16),
            pltpu.VMEM((FACES, block, elements), BF16),
            pltpu.VMEM((n_sub, 2, block, 2 * cap), BF16),
            pltpu.VMEM((n_sub, 2, block, 2 * cap), BF16),
            pltpu.VMEM((2, block, span_group), BF16),
            pltpu.VMEM((2, block, span_group), BF16),
            pltpu.VMEM((4, far_tiles * block, SPAN), BF16),
            dma((tiles,)), dma((n_sub,)), dma((n_sub,)), dma((2,)), dma((2,)),
        ],
        compiler_params=pltpu.CompilerParams(
            collective_id=0, has_side_effects=True, vmem_limit_bytes=56 * 2**20),
        name="flux",
    )(adjoint, face_speed, neighbours, sub_sends, group_sends, select, spread)

    tile_count = tile_slot.shape[0]
    heights = emission_profile.shape[1]
    whole = lambda shape: pl.BlockSpec(shape, lambda i: (0,) * len(shape))
    along = lambda *lead: pl.BlockSpec(lead + (WIDE,), lambda i: (0,) * len(lead) + (i,))
    slots = tile_slot.reshape(tile_count // 128, 128)
    adjoint_next, partial = pl.pallas_call(
        step_kernel,
        grid=(elements // WIDE,),
        out_shape=(
            jax.ShapeDtypeStruct(adjoint.shape, F32),
            jax.ShapeDtypeStruct((tile_count, species * heights), F32),
        ),
        in_specs=[
            along(species, nodes), along(velocity.shape[0], nodes), along(species, FACES * pad),
            whole(derivatives.shape), whole(lift_operator.shape[::-1]), whole(emission_profile.shape[::-1]),
            whole(spread.shape), along(1), whole(slots.shape),
        ],
        out_specs=(along(species, nodes), whole((tile_count, species * heights))),
        scratch_shapes=[pltpu.VMEM((nodes, FACES * pad), BF16)],
        compiler_params=pltpu.CompilerParams(vmem_limit_bytes=56 * 2**20),
        name="step",
    )(
        adjoint, velocity, flux, derivatives, lift_operator.T, emission_profile.T,
        spread, element_tile.reshape(1, elements), slots,
    )

    own = tile_count // (n_group * n_sub)
    width = species * heights
    emission_grad = pl.pallas_call(
        functools.partial(sum_kernel, n_group, n_sub),
        out_shape=jax.ShapeDtypeStruct((own, width), F32),
        in_specs=[pl.BlockSpec(memory_space=pl.ANY)],
        out_specs=vmem,
        scratch_shapes=[
            pltpu.VMEM((tile_count, width), F32),
            pltpu.VMEM((n_sub, n_group, own, width), BF16),
            pltpu.VMEM((n_sub, n_group, own, width), BF16),
            pltpu.VMEM((n_group, own, width), F32),
            pltpu.VMEM((n_group, own, width), F32),
            dma, dma((n_sub,)), dma((n_sub,)), dma((n_group,)), dma((n_group,)),
        ],
        compiler_params=pltpu.CompilerParams(
            collective_id=1, has_side_effects=True, vmem_limit_bytes=56 * 2**20),
        name="sum",
    )(partial)
    return adjoint_next, emission_grad


def solution(mesh):
    both = ("group", "sub")
    placed = (
        P(None, None, both), P(None, None, both), P(None, both), P(), P(), P(),
        P(None, both), P(None, both), P(None, both), P(both), P(),
    )
    return jax.shard_map(
        functools.partial(on_device, mesh.shape["group"], mesh.shape["sub"]),
        mesh=mesh,
        in_specs=placed,
        out_specs=(P(None, None, both), P(both, None)),
        check_vma=False,
    )
```

```python
import functools

import jax
import jax.numpy as jnp
import numpy as np
from jax import lax
from jax.experimental import pallas as pl
from jax.experimental.pallas import tpu as pltpu
from jax.sharding import PartitionSpec as P

ORDER = 5
SECTION = 0.125
FACES = 6
SPAN = 256
WIDE = 512
STRIP = 16
MESH = pl.DeviceIdType.MESH
F32, BF16 = jnp.float32, jnp.bfloat16


def face_table(order):
    edge = order + 1
    a, b = np.meshgrid(np.arange(edge), np.arange(edge), indexing="ij")
    a, b = a.reshape(-1), b.reshape(-1)
    rows = []
    for axis_id in range(3):
        for level in (0, edge - 1):
            fixed = a * 0 + level
            i, j, l = [(fixed, a, b), (a, fixed, b), (a, b, fixed)][axis_id]
            rows.append((i * edge + j) * edge + l)
    return np.stack(rows).astype(np.int32)


def padded_nodes(face_nodes):
    return -(-face_nodes // 8) * 8


def select_matrix(node_count):
    table = face_table(ORDER)
    pad = padded_nodes(table.shape[1])
    out = np.zeros((FACES * pad, node_count), np.float32)
    for f in range(FACES):
        for k, n in enumerate(table[f]):
            out[f * pad + k, n] = 1
    return out


def spread_matrix(face_nodes):
    pad = padded_nodes(face_nodes)
    out = np.zeros((FACES * pad, FACES * face_nodes), np.float32)
    for f in range(FACES):
        for k in range(face_nodes):
            out[f * pad + k, f * face_nodes + k] = 1
    return out


def dot(a, b):
    return jnp.dot(a, b, preferred_element_type=F32)


def dot_nt(a, b):
    return lax.dot_general(a, b, (((1,), (1,)), ((), ())), preferred_element_type=F32)


def one_hot_rows(index, rows):
    ids = lax.broadcasted_iota(jnp.int32, (rows, index.shape[1]), 0).astype(jnp.int16)
    return jnp.where(ids == index.astype(jnp.int16), jnp.ones((), BF16), jnp.zeros((), BF16))


def columns_of(stack, position, first, count, block, picked, emit):
    picked[: count * block, :] = dot(stack, one_hot_rows(position & (SPAN - 1), SPAN))
    tile = jnp.broadcast_to(position >> (SPAN.bit_length() - 1), (STRIP, position.shape[1]))
    for r in range(0, block, STRIP):
        rows = picked[r : r + STRIP, :]
        for t in range(1, count):
            rows = jnp.where(tile == first + t, picked[t * block + r : t * block + r + STRIP, :], rows)
        emit(r, rows)


def flux_kernel(
    n_group, n_sub, cap,
    adjoint, speed, neighbours, sub_sends, group_sends, select, spread,
    flux,
    field, table, local, send_sub, recv_sub, send_group, recv_group, far_sub,
    picked, upwind, flux_wide, flux_out,
    field_sem, flux_sem, sub_send_sem, sub_recv_sem, group_send_sem, group_recv_sem,
):
    tiles, species = field.shape[0], field.shape[1]
    pad = select.shape[0] // FACES
    block = species * pad
    elements = tiles * SPAN
    g, q = lax.axis_index("group"), lax.axis_index("sub")
    above = (lax.rem(g + 1, n_group), q)
    below = (lax.rem(g + n_group - 1, n_group), q)

    def field_copy(i):
        cols = pl.ds(pl.multiple_of(i * SPAN, SPAN), SPAN)
        return pltpu.make_async_copy(adjoint.at[:, :, cols], field.at[i], field_sem.at[i])

    for i in range(tiles):
        field_copy(i).start()

    barrier = pltpu.get_barrier_semaphore()
    peers = [(g, lax.rem(q + d, n_sub)) for d in range(1, n_sub)] + [above, below]
    for peer in peers:
        pl.semaphore_signal(barrier, inc=1, device_id=peer, device_id_type=MESH)

    def trace_tile(i, carry):
        for j in range(WIDE // SPAN):
            field_copy(i * (WIDE // SPAN) + j).wait()
        for j in range(WIDE // SPAN):
            tile = i * (WIDE // SPAN) + j
            parts = [dot(select[...], field[tile, s].astype(BF16)) for s in range(species)]
            rows = pl.ds(pl.multiple_of(tile * block, block), block)
            for f in range(FACES):
                one = jnp.concatenate([p[f * pad : (f + 1) * pad] for p in parts], axis=0)
                table[f, rows, :] = one.astype(BF16)
        return carry

    lax.fori_loop(0, tiles * SPAN // WIDE, trace_tile, 0)

    low_half = lax.broadcasted_iota(jnp.int32, (STRIP, 2 * cap), 1) < cap
    for axis_id in range(2):
        for c in range(n_sub * cap // WIDE):
            cols = slice(c * WIDE, (c + 1) * WIDE)
            def keep(r, rows):
                flux_wide[0, r : r + STRIP, :] = rows

            def merge(r, plus):
                minus = flux_wide[0, r : r + STRIP, :]
                for m in range(WIDE // (2 * cap)):
                    part = slice(m * 2 * cap, (m + 1) * 2 * cap)
                    a, b = minus[:, part], plus[:, part]
                    to = c * (WIDE // cap) + 2 * m
                    send_sub[to, axis_id, r : r + STRIP, :] = jnp.where(
                        low_half, a, pltpu.roll(b, cap, 1)).astype(BF16)
                    send_sub[to + 1, axis_id, r : r + STRIP, :] = jnp.where(
                        low_half, pltpu.roll(a, cap, 1), b).astype(BF16)

            for k, emit in ((0, keep), (1, merge)):
                f = 2 * axis_id + k
                columns_of(table[f], sub_sends[f : f + 1, cols], 0, tiles, block, picked.at[k], emit)
    pl.semaphore_wait(barrier, len(peers))
    copies = []
    for d in range(1, n_sub):
        peer = lax.rem(q + d, n_sub)
        copies.append(
            pltpu.make_async_remote_copy(
                src_ref=send_sub.at[peer], dst_ref=recv_sub.at[q],
                send_sem=sub_send_sem.at[d], recv_sem=sub_recv_sem.at[d],
                device_id=(g, peer), device_id_type=MESH,
            )
        )
        copies[-1].start()
    span_group = send_group.shape[2]
    for k, target in ((0, below), (1, above)):
        for c in range(span_group // SPAN):
            cols = slice(c * SPAN, (c + 1) * SPAN)

            def keep(r, rows):
                send_group[k, r : r + STRIP, cols] = rows.astype(BF16)

            columns_of(
                table[4 + k], group_sends[k : k + 1, cols], 0, tiles, block,
                picked.at[k, :, :SPAN], keep)
        copies.append(
            pltpu.make_async_remote_copy(
                src_ref=send_group.at[k], dst_ref=recv_group.at[k],
                send_sem=group_send_sem.at[k], recv_sem=group_recv_sem.at[k],
                device_id=target, device_id_type=MESH,
            )
        )
        copies[-1].start()
    recv_sub[q] = jnp.zeros(recv_sub.shape[1:], BF16)

    def local_tile(i, carry):
        cols = pl.ds(pl.multiple_of(i * WIDE, WIDE), WIDE)
        for f in range(FACES):

            def keep(r, rows):
                local[f, r : r + STRIP, cols] = rows.astype(BF16)

            columns_of(
                table[f ^ 1], neighbours[f : f + 1, cols], 0, tiles, block, picked.at[f % 2], keep)
        return carry

    lax.fori_loop(0, elements // WIDE, local_tile, 0)

    for copy in copies:
        copy.wait()
    far_tiles = n_sub * cap // SPAN
    for t in range(4):
        for r in range(0, n_sub, 2):
            lane = r * cap
            for k in range(0, block, STRIP):
                a = recv_sub[r, t // 2, k : k + STRIP, :].astype(F32)
                b = recv_sub[r + 1, t // 2, k : k + STRIP, :].astype(F32)
                if t % 2 == 0:
                    both = jnp.where(low_half, a, pltpu.roll(b, cap, 1))
                else:
                    both = jnp.where(low_half, pltpu.roll(a, cap, 1), b)
                row = (lane // SPAN) * block + k
                far_sub[t, row : row + STRIP, lane % SPAN : lane % SPAN + 2 * cap] = both.astype(BF16)

    def flux_copy(i):
        cols = pl.ds(pl.multiple_of(i * WIDE, WIDE), WIDE)
        return pltpu.make_async_copy(flux_out.at[i], flux.at[:, :, cols], flux_sem.at[i])

    def flux_tile(i, carry):
        cols = pl.ds(pl.multiple_of(i * WIDE, WIDE), WIDE)
        inside = WIDE // SPAN
        upwind[...] = jnp.maximum(dot(spread[...], speed[:, cols]), 0.0)
        for f in range(FACES):
            t = f ^ 1
            position = neighbours[f : f + 1, cols]
            remote = jnp.broadcast_to(position, (STRIP, WIDE)) >= elements

            def keep(r, far):
                outside = jnp.where(remote, far, local[f, r : r + STRIP, cols].astype(F32))
                here = jnp.concatenate([
                    table[f, pl.ds(pl.multiple_of((i * inside + j) * block + r, STRIP), STRIP), :]
                    for j in range(inside)
                ], axis=1)
                jump = outside - here.astype(F32)
                for h in range(0, STRIP, 8):
                    s, k = (r + h) // pad, (r + h) % pad
                    row = f * pad + k
                    flux_wide[s, row : row + 8, :] = upwind[row : row + 8, :] * jump[h : h + 8]

            if t < 4:
                stack, first, count = far_sub[t], tiles, far_tiles
            else:
                first, count = tiles + far_tiles, span_group // SPAN
                stack = jnp.concatenate([
                    recv_group[t - 4, :, c * SPAN : (c + 1) * SPAN] for c in range(count)
                ], axis=0)
            columns_of(stack, position, first, count, block, picked.at[f % 2], keep)
        for s in range(species):
            for r in range(0, FACES * pad, STRIP):
                flux_out[i, s, r : r + STRIP, :] = flux_wide[s, r : r + STRIP, :].astype(BF16)
        flux_copy(i).start()
        return carry

    lax.fori_loop(0, elements // WIDE, flux_tile, 0)
    for i in range(elements // WIDE):
        flux_copy(i).wait()


def step_kernel(
    adjoint, velocity, flux, derivatives, lift, profile, spread, element_tile, tile_slot,
    adjoint_next, partial, lift_wide, grads, lifted, next_low,
):
    species, nodes, span = adjoint.shape
    tile_rows = partial.shape[0]

    @pl.when(pl.program_id(0) == 0)
    def _():
        lift_wide[...] = dot(spread[...], lift[...]).T.astype(BF16)
        partial[...] = jnp.zeros_like(partial)

    tile = element_tile[...]
    width = tile_slot.shape[1]
    slots = tile_slot[...]
    high = dot((slots >> 8).astype(F32).astype(BF16), one_hot_rows(lax.rem(tile, width), width))
    low = dot((slots & 255).astype(F32).astype(BF16), one_hot_rows(lax.rem(tile, width), width))
    picked = (high * 256.0 + low)
    which = lax.broadcasted_iota(jnp.int32, picked.shape, 0) == lax.div(tile, width)
    row = jnp.sum(jnp.where(which, picked, 0.0), axis=0, keepdims=True).astype(jnp.int32)

    contrib = []
    for s in range(species):
        slot = s % 2
        grads[slot] = dot(derivatives[...], adjoint[s].astype(BF16))
        lifted[slot] = dot(lift_wide[...], flux[s])
        for r in range(0, nodes, STRIP):
            rows = slice(r, r + STRIP)
            total = lifted[slot, rows, :]
            for d in range(3):
                wind = velocity[d, rows, :].astype(F32)
                total += wind * grads[slot, d * nodes + r : d * nodes + r + STRIP, :]
            result = adjoint[s, rows, :] + SECTION * total
            adjoint_next[s, rows, :] = result
            next_low[slot, rows, :] = result.astype(BF16)
        contrib.append(dot(profile[...], next_low[slot]))
    terms = jnp.concatenate(contrib, axis=0)
    first = terms.astype(BF16)
    second = (terms - first.astype(F32)).astype(BF16)
    both = jnp.concatenate([first, second], axis=0)
    sums = dot_nt(one_hot_rows(row, tile_rows), both)
    half = terms.shape[0]
    partial[...] += sums[:, :half] + sums[:, half:]


def sum_kernel(
    n_group, n_sub,
    partial_hbm, out,
    partial, send, recv, mid, recv_mid,
    load_sem, send_sem, recv_sem, mid_send_sem, mid_recv_sem,
):
    load = pltpu.make_async_copy(partial_hbm, partial, load_sem)
    load.start()
    own = out.shape[0]
    g, q = lax.axis_index("group"), lax.axis_index("sub")
    barrier = pltpu.get_barrier_semaphore()
    peers = [(g, lax.rem(q + d, n_sub)) for d in range(1, n_sub)]
    peers += [(lax.rem(g + d, n_group), q) for d in range(1, n_group)]
    for peer in peers:
        pl.semaphore_signal(barrier, inc=1, device_id=peer, device_id_type=MESH)

    def rows_of(group, sub):
        return pl.ds(pl.multiple_of((group * n_sub + sub) * own, own), own)

    load.wait()
    order = sorted(range(1, n_group), key=lambda d: -min(d, n_group - d)) + [0]
    for e, step in enumerate(order):
        k = lax.rem(g + step, n_group)
        for d in range(1, n_sub):
            send[e, d] = partial[rows_of(k, lax.rem(q + d, n_sub)), :].astype(BF16)
    pl.semaphore_wait(barrier, len(peers))
    first = []
    for e in range(n_group):
        for d in range(1, n_sub):
            copy = pltpu.make_async_remote_copy(
                src_ref=send.at[e, d], dst_ref=recv.at[e, d],
                send_sem=send_sem.at[e, d], recv_sem=recv_sem.at[e, d],
                device_id=(g, lax.rem(q + d, n_sub)), device_id_type=MESH,
            )
            copy.start()
            first.append(copy)
    second = []
    for e, step in enumerate(order):
        k = lax.rem(g + step, n_group)
        total = partial[rows_of(k, q), :]
        for d in range(1, n_sub):
            first[e * (n_sub - 1) + d - 1].wait_recv()
            total += recv[e, d].astype(F32)
        if step == 0:
            break
        mid[e] = total
        copy = pltpu.make_async_remote_copy(
            src_ref=mid.at[e], dst_ref=recv_mid.at[e],
            send_sem=mid_send_sem.at[e], recv_sem=mid_recv_sem.at[e],
            device_id=(k, q), device_id_type=MESH,
        )
        copy.start()
        second.append(copy)
    for e, copy in enumerate(second):
        copy.wait_recv()
        total += recv_mid[e]
    out[...] = total
    for copy in first + second:
        copy.wait_send()


def on_device(
    n_group, n_sub,
    adjoint, velocity, face_speed, derivatives, lift_operator, emission_profile,
    neighbours, sub_sends, group_sends, element_tile, tile_slot,
):
    species, nodes, elements = adjoint.shape
    face_nodes = face_speed.shape[0] // FACES
    pad = padded_nodes(face_nodes)
    block = species * pad
    tiles = elements // SPAN
    cap = sub_sends.shape[1] // n_sub
    span_group = group_sends.shape[1]
    assert elements % WIDE == 0 and n_sub * cap % WIDE == 0 and SPAN % (2 * cap) == 0 and 2 * cap == 128
    assert (n_sub * cap) % SPAN == 0 and span_group % SPAN == 0
    select = jnp.asarray(select_matrix(nodes), BF16)
    spread = jnp.asarray(spread_matrix(face_nodes), BF16)
    vmem = pl.BlockSpec(memory_space=pltpu.VMEM)
    dma = pltpu.SemaphoreType.DMA
    far_tiles = n_sub * cap // SPAN

    flux = pl.pallas_call(
        functools.partial(flux_kernel, n_group, n_sub, cap),
        out_shape=jax.ShapeDtypeStruct((species, FACES * pad, elements), BF16),
        in_specs=[pl.BlockSpec(memory_space=pl.ANY)] + [vmem] * 6,
        out_specs=pl.BlockSpec(memory_space=pl.ANY),
        scratch_shapes=[
            pltpu.VMEM((tiles, species, nodes, SPAN), F32),
            pltpu.VMEM((FACES, tiles * block, SPAN), BF16),
            pltpu.VMEM((FACES, block, elements), BF16),
            pltpu.VMEM((n_sub, 2, block, 2 * cap), BF16),
            pltpu.VMEM((n_sub, 2, block, 2 * cap), BF16),
            pltpu.VMEM((2, block, span_group), BF16),
            pltpu.VMEM((2, block, span_group), BF16),
            pltpu.VMEM((4, far_tiles * block, SPAN), BF16),
            pltpu.VMEM((2, max(tiles, far_tiles) * block, WIDE), F32),
            pltpu.VMEM((FACES * pad, WIDE), F32),
            pltpu.VMEM((species, FACES * pad, WIDE), F32),
            pltpu.VMEM((elements // WIDE, species, FACES * pad, WIDE), BF16),
            dma((tiles,)), dma((elements // WIDE,)),
            dma((n_sub,)), dma((n_sub,)), dma((2,)), dma((2,)),
        ],
        compiler_params=pltpu.CompilerParams(
            collective_id=0, has_side_effects=True, vmem_limit_bytes=56 * 2**20),
        name="flux",
    )(adjoint, face_speed, neighbours, sub_sends, group_sends, select, spread)

    tile_count = tile_slot.shape[0]
    heights = emission_profile.shape[1]
    whole = lambda shape: pl.BlockSpec(shape, lambda i: (0,) * len(shape))
    along = lambda *lead: pl.BlockSpec(lead + (WIDE,), lambda i: (0,) * len(lead) + (i,))
    slots = tile_slot.reshape(tile_count // 128, 128)
    adjoint_next, partial = pl.pallas_call(
        step_kernel,
        grid=(elements // WIDE,),
        out_shape=(
            jax.ShapeDtypeStruct(adjoint.shape, F32),
            jax.ShapeDtypeStruct((tile_count, species * heights), F32),
        ),
        in_specs=[
            along(species, nodes), along(velocity.shape[0], nodes), along(species, FACES * pad),
            whole(derivatives.shape), whole(lift_operator.shape[::-1]), whole(emission_profile.shape[::-1]),
            whole(spread.shape), along(1), whole(slots.shape),
        ],
        out_specs=(along(species, nodes), whole((tile_count, species * heights))),
        scratch_shapes=[
            pltpu.VMEM((nodes, FACES * pad), BF16),
            pltpu.VMEM((2, 3 * nodes, WIDE), F32),
            pltpu.VMEM((2, nodes, WIDE), F32),
            pltpu.VMEM((2, nodes, WIDE), BF16),
        ],
        compiler_params=pltpu.CompilerParams(vmem_limit_bytes=56 * 2**20),
        name="step",
    )(
        adjoint, velocity, flux, derivatives, lift_operator.T, emission_profile.T,
        spread, element_tile.reshape(1, elements), slots,
    )

    own = tile_count // (n_group * n_sub)
    width = species * heights
    emission_grad = pl.pallas_call(
        functools.partial(sum_kernel, n_group, n_sub),
        out_shape=jax.ShapeDtypeStruct((own, width), F32),
        in_specs=[pl.BlockSpec(memory_space=pl.ANY)],
        out_specs=vmem,
        scratch_shapes=[
            pltpu.VMEM((tile_count, width), F32),
            pltpu.VMEM((n_group, n_sub, own, width), BF16),
            pltpu.VMEM((n_group, n_sub, own, width), BF16),
            pltpu.VMEM((n_group, own, width), F32),
            pltpu.VMEM((n_group, own, width), F32),
            dma, dma((n_group, n_sub)), dma((n_group, n_sub)), dma((n_group,)), dma((n_group,)),
        ],
        compiler_params=pltpu.CompilerParams(
            collective_id=1, has_side_effects=True, vmem_limit_bytes=56 * 2**20),
        name="sum",
    )(partial)
    return adjoint_next, emission_grad


def solution(mesh):
    both = ("group", "sub")
    placed = (
        P(None, None, both), P(None, None, both), P(None, both), P(), P(), P(),
        P(None, both), P(None, both), P(None, both), P(both), P(),
    )
    return jax.shard_map(
        functools.partial(on_device, mesh.shape["group"], mesh.shape["sub"]),
        mesh=mesh,
        in_specs=placed,
        out_specs=(P(None, None, both), P(both, None)),
        check_vma=False,
    )
```

```python
import functools

import jax
import jax.numpy as jnp
import numpy as np
from jax import lax
from jax.experimental import pallas as pl
from jax.experimental.pallas import tpu as pltpu
from jax.sharding import PartitionSpec as P

ORDER = 5
SECTION = 0.125
FACES = 6
SPAN = 256
WIDE = 512
MESH = pl.DeviceIdType.MESH
F32, BF16 = jnp.float32, jnp.bfloat16


def face_table(order):
    edge = order + 1
    a, b = np.meshgrid(np.arange(edge), np.arange(edge), indexing="ij")
    a, b = a.reshape(-1), b.reshape(-1)
    rows = []
    for axis_id in range(3):
        for level in (0, edge - 1):
            fixed = a * 0 + level
            i, j, l = [(fixed, a, b), (a, fixed, b), (a, b, fixed)][axis_id]
            rows.append((i * edge + j) * edge + l)
    return np.stack(rows).astype(np.int32)


def padded_nodes(face_nodes):
    return -(-face_nodes // 8) * 8


def select_matrix(node_count):
    table = face_table(ORDER)
    pad = padded_nodes(table.shape[1])
    out = np.zeros((FACES * pad, node_count), np.float32)
    for f in range(FACES):
        for k, n in enumerate(table[f]):
            out[f * pad + k, n] = 1
    return out


def spread_matrix(face_nodes):
    pad = padded_nodes(face_nodes)
    out = np.zeros((FACES * pad, FACES * face_nodes), np.float32)
    for f in range(FACES):
        for k in range(face_nodes):
            out[f * pad + k, f * face_nodes + k] = 1
    return out


def dot(a, b):
    return jnp.dot(a, b, preferred_element_type=F32)


def dot_nt(a, b):
    return lax.dot_general(a, b, (((1,), (1,)), ((), ())), preferred_element_type=F32)


def one_hot_rows(index, rows):
    ids = lax.broadcasted_iota(jnp.int32, (rows, index.shape[1]), 0).astype(jnp.int16)
    return jnp.where(ids == index.astype(jnp.int16), jnp.ones((), BF16), jnp.zeros((), BF16))


def columns_of(stack, position, first, count, block):
    picked = dot(stack, one_hot_rows(position & (SPAN - 1), SPAN))
    tile = position >> (SPAN.bit_length() - 1)
    out = picked[:block]
    for t in range(1, count):
        out = jnp.where(tile == first + t, picked[t * block : (t + 1) * block], out)
    return out


def flux_kernel(
    n_group, n_sub, cap,
    adjoint, speed, neighbours, sub_sends, group_sends, select, spread,
    flux,
    field, table, local, send_sub, recv_sub, send_group, recv_group, far_sub,
    field_sem, sub_send_sem, sub_recv_sem, group_send_sem, group_recv_sem,
):
    tiles, species = field.shape[0], field.shape[1]
    pad = select.shape[0] // FACES
    block = species * pad
    elements = tiles * SPAN
    g, q = lax.axis_index("group"), lax.axis_index("sub")
    above = (lax.rem(g + 1, n_group), q)
    below = (lax.rem(g + n_group - 1, n_group), q)

    def field_copy(i):
        cols = pl.ds(pl.multiple_of(i * SPAN, SPAN), SPAN)
        return pltpu.make_async_copy(adjoint.at[:, :, cols], field.at[i], field_sem.at[i])

    for i in range(tiles):
        field_copy(i).start()

    barrier = pltpu.get_barrier_semaphore()
    peers = [(g, lax.rem(q + d, n_sub)) for d in range(1, n_sub)] + [above, below]
    for peer in peers:
        pl.semaphore_signal(barrier, inc=1, device_id=peer, device_id_type=MESH)

    def trace_tile(i, carry):
        for j in range(WIDE // SPAN):
            field_copy(i * (WIDE // SPAN) + j).wait()
        for j in range(WIDE // SPAN):
            tile = i * (WIDE // SPAN) + j
            parts = [dot(select[...], field[tile, s].astype(BF16)) for s in range(species)]
            rows = pl.ds(pl.multiple_of(tile * block, block), block)
            for f in range(FACES):
                one = jnp.concatenate([p[f * pad : (f + 1) * pad] for p in parts], axis=0)
                table[f, rows, :] = one.astype(BF16)
        return carry

    lax.fori_loop(0, tiles * SPAN // WIDE, trace_tile, 0)

    low_half = lax.broadcasted_iota(jnp.int32, (block, 2 * cap), 1) < cap
    for axis_id in range(2):
        for c in range(n_sub * cap // WIDE):
            cols = slice(c * WIDE, (c + 1) * WIDE)
            minus, plus = [
                columns_of(table[f], sub_sends[f : f + 1, cols], 0, tiles, block)
                for f in (2 * axis_id, 2 * axis_id + 1)
            ]
            for m in range(WIDE // (2 * cap)):
                part = slice(m * 2 * cap, (m + 1) * 2 * cap)
                a, b = minus[:, part], plus[:, part]
                r = c * (WIDE // cap) + 2 * m
                send_sub[r, axis_id] = jnp.where(low_half, a, pltpu.roll(b, cap, 1)).astype(BF16)
                send_sub[r + 1, axis_id] = jnp.where(low_half, pltpu.roll(a, cap, 1), b).astype(BF16)
    pl.semaphore_wait(barrier, len(peers))
    copies = []
    for d in range(1, n_sub):
        peer = lax.rem(q + d, n_sub)
        copies.append(
            pltpu.make_async_remote_copy(
                src_ref=send_sub.at[peer], dst_ref=recv_sub.at[q],
                send_sem=sub_send_sem.at[d], recv_sem=sub_recv_sem.at[d],
                device_id=(g, peer), device_id_type=MESH,
            )
        )
        copies[-1].start()
    span_group = send_group.shape[2]
    for k, target in ((0, below), (1, above)):
        for c in range(span_group // SPAN):
            cols = slice(c * SPAN, (c + 1) * SPAN)
            got = columns_of(table[4 + k], group_sends[k : k + 1, cols], 0, tiles, block)
            send_group[k, :, cols] = got.astype(BF16)
        copies.append(
            pltpu.make_async_remote_copy(
                src_ref=send_group.at[k], dst_ref=recv_group.at[k],
                send_sem=group_send_sem.at[k], recv_sem=group_recv_sem.at[k],
                device_id=target, device_id_type=MESH,
            )
        )
        copies[-1].start()
    recv_sub[q] = jnp.zeros(recv_sub.shape[1:], BF16)

    def local_tile(i, carry):
        cols = pl.ds(pl.multiple_of(i * WIDE, WIDE), WIDE)
        for f in range(FACES):
            got = columns_of(table[f ^ 1], neighbours[f : f + 1, cols], 0, tiles, block)
            local[f, :, cols] = got.astype(BF16)
        return carry

    lax.fori_loop(0, elements // WIDE, local_tile, 0)

    for copy in copies:
        copy.wait()
    far_tiles = n_sub * cap // SPAN
    for t in range(4):
        for r in range(0, n_sub, 2):
            a = recv_sub[r, t // 2].astype(F32)
            b = recv_sub[r + 1, t // 2].astype(F32)
            if t % 2 == 0:
                both = jnp.where(low_half, a, pltpu.roll(b, cap, 1))
            else:
                both = jnp.where(low_half, pltpu.roll(a, cap, 1), b)
            lane = r * cap
            far_sub[t, (lane // SPAN) * block : (lane // SPAN + 1) * block,
                    lane % SPAN : lane % SPAN + 2 * cap] = both.astype(BF16)

    def flux_tile(i, carry):
        cols = pl.ds(pl.multiple_of(i * WIDE, WIDE), WIDE)
        inside = WIDE // SPAN
        upwind = jnp.maximum(dot(spread[...], speed[:, cols]), 0.0)
        parts = []
        for f in range(FACES):
            t = f ^ 1
            position = neighbours[f : f + 1, cols]
            if t < 4:
                far = columns_of(far_sub[t], position, tiles, far_tiles, block)
            else:
                stack = jnp.concatenate([
                    recv_group[t - 4, :, c * SPAN : (c + 1) * SPAN]
                    for c in range(span_group // SPAN)
                ], axis=0)
                far = columns_of(stack, position, tiles + far_tiles, span_group // SPAN, block)
            outside = jnp.where(position >= elements, far, local[f, :, cols].astype(F32))
            wind = jnp.concatenate([upwind[f * pad : (f + 1) * pad]] * species, axis=0)
            here = jnp.concatenate([
                table[f, pl.ds(pl.multiple_of((i * inside + j) * block, block), block), :]
                for j in range(inside)
            ], axis=1)
            parts.append(wind * (outside - here.astype(F32)))
        for s in range(species):
            one = jnp.concatenate([p[s * pad : (s + 1) * pad] for p in parts], axis=0)
            flux[s, :, cols] = one.astype(BF16)
        return carry

    lax.fori_loop(0, elements // WIDE, flux_tile, 0)


def step_kernel(
    adjoint, velocity, flux, derivatives, lift, profile, spread, element_tile, tile_slot,
    adjoint_next, partial, lift_wide,
):
    species, nodes, span = adjoint.shape
    tile_rows = partial.shape[0]

    @pl.when(pl.program_id(0) == 0)
    def _():
        lift_wide[...] = dot(spread[...], lift[...]).T.astype(BF16)
        partial[...] = jnp.zeros_like(partial)

    tile = element_tile[...]
    width = tile_slot.shape[1]
    slots = tile_slot[...]
    high = dot((slots >> 8).astype(F32).astype(BF16), one_hot_rows(lax.rem(tile, width), width))
    low = dot((slots & 255).astype(F32).astype(BF16), one_hot_rows(lax.rem(tile, width), width))
    picked = (high * 256.0 + low)
    which = lax.broadcasted_iota(jnp.int32, picked.shape, 0) == lax.div(tile, width)
    row = jnp.sum(jnp.where(which, picked, 0.0), axis=0, keepdims=True).astype(jnp.int32)

    contrib = []
    wind = [velocity[d].astype(F32) for d in range(3)]
    for s in range(species):
        field = adjoint[s]
        grads = dot(derivatives[...], field.astype(BF16))
        total = dot(lift_wide[...], flux[s])
        for d in range(3):
            total += wind[d] * grads[d * nodes : (d + 1) * nodes]
        result = field + SECTION * total
        adjoint_next[s] = result
        contrib.append(dot(profile[...], result.astype(BF16)))
    terms = jnp.concatenate(contrib, axis=0)
    first = terms.astype(BF16)
    second = (terms - first.astype(F32)).astype(BF16)
    both = jnp.concatenate([first, second], axis=0)
    sums = dot_nt(one_hot_rows(row, tile_rows), both)
    half = terms.shape[0]
    partial[...] += sums[:, :half] + sums[:, half:]


def sum_kernel(
    n_group, n_sub,
    partial, out,
    send, recv, mid, recv_mid,
    send_sem, recv_sem, mid_send_sem, mid_recv_sem,
):
    own = out.shape[0]
    g, q = lax.axis_index("group"), lax.axis_index("sub")
    barrier = pltpu.get_barrier_semaphore()
    peers = [(g, lax.rem(q + d, n_sub)) for d in range(1, n_sub)]
    peers += [(lax.rem(g + d, n_group), q) for d in range(1, n_group)]
    for peer in peers:
        pl.semaphore_signal(barrier, inc=1, device_id=peer, device_id_type=MESH)

    def rows_of(group, sub):
        return pl.ds(pl.multiple_of((group * n_sub + sub) * own, own), own)

    for d in range(1, n_sub):
        for k in range(n_group):
            send[d, k] = partial[rows_of(k, lax.rem(q + d, n_sub)), :].astype(BF16)
    pl.semaphore_wait(barrier, len(peers))
    copies = []
    for d in range(1, n_sub):
        copies.append(
            pltpu.make_async_remote_copy(
                src_ref=send.at[d], dst_ref=recv.at[d],
                send_sem=send_sem.at[d], recv_sem=recv_sem.at[d],
                device_id=(g, lax.rem(q + d, n_sub)), device_id_type=MESH,
            )
        )
        copies[-1].start()
    for k in range(n_group):
        mid[k] = partial[rows_of(k, q), :]
    for copy in copies:
        copy.wait()
    for k in range(n_group):
        total = mid[k]
        for d in range(1, n_sub):
            total += recv[d, k].astype(F32)
        mid[k] = total
    copies = []
    for d in range(1, n_group):
        other = lax.rem(g + d, n_group)
        copies.append(
            pltpu.make_async_remote_copy(
                src_ref=mid.at[other], dst_ref=recv_mid.at[d],
                send_sem=mid_send_sem.at[d], recv_sem=mid_recv_sem.at[d],
                device_id=(other, q), device_id_type=MESH,
            )
        )
        copies[-1].start()
    for copy in copies:
        copy.wait()
    total = mid[g]
    for d in range(1, n_group):
        total += recv_mid[d]
    out[...] = total


def on_device(
    n_group, n_sub,
    adjoint, velocity, face_speed, derivatives, lift_operator, emission_profile,
    neighbours, sub_sends, group_sends, element_tile, tile_slot,
):
    species, nodes, elements = adjoint.shape
    face_nodes = face_speed.shape[0] // FACES
    pad = padded_nodes(face_nodes)
    block = species * pad
    tiles = elements // SPAN
    cap = sub_sends.shape[1] // n_sub
    span_group = group_sends.shape[1]
    assert elements % WIDE == 0 and n_sub * cap % WIDE == 0 and SPAN % (2 * cap) == 0 and 2 * cap == 128
    assert (n_sub * cap) % SPAN == 0 and span_group % SPAN == 0
    select = jnp.asarray(select_matrix(nodes), BF16)
    spread = jnp.asarray(spread_matrix(face_nodes), BF16)
    vmem = pl.BlockSpec(memory_space=pltpu.VMEM)
    dma = pltpu.SemaphoreType.DMA
    far_tiles = n_sub * cap // SPAN

    flux = pl.pallas_call(
        functools.partial(flux_kernel, n_group, n_sub, cap),
        out_shape=jax.ShapeDtypeStruct((species, FACES * pad, elements), BF16),
        in_specs=[pl.BlockSpec(memory_space=pltpu.HBM)] + [vmem] * 6,
        out_specs=vmem,
        scratch_shapes=[
            pltpu.VMEM((tiles, species, nodes, SPAN), F32),
            pltpu.VMEM((FACES, tiles * block, SPAN), BF16),
            pltpu.VMEM((FACES, block, elements), BF16),
            pltpu.VMEM((n_sub, 2, block, 2 * cap), BF16),
            pltpu.VMEM((n_sub, 2, block, 2 * cap), BF16),
            pltpu.VMEM((2, block, span_group), BF16),
            pltpu.VMEM((2, block, span_group), BF16),
            pltpu.VMEM((4, far_tiles * block, SPAN), BF16),
            dma((tiles,)), dma((n_sub,)), dma((n_sub,)), dma((2,)), dma((2,)),
        ],
        compiler_params=pltpu.CompilerParams(
            collective_id=0, has_side_effects=True, vmem_limit_bytes=46 * 2**20),
        name="flux",
    )(adjoint, face_speed, neighbours, sub_sends, group_sends, select, spread)

    tile_count = tile_slot.shape[0]
    heights = emission_profile.shape[1]
    whole = lambda shape: pl.BlockSpec(shape, lambda i: (0,) * len(shape))
    along = lambda *lead: pl.BlockSpec(lead + (WIDE,), lambda i: (0,) * len(lead) + (i,))
    slots = tile_slot.reshape(tile_count // 128, 128)
    adjoint_next, partial = pl.pallas_call(
        step_kernel,
        grid=(elements // WIDE,),
        out_shape=(
            jax.ShapeDtypeStruct(adjoint.shape, F32),
            jax.ShapeDtypeStruct((tile_count, species * heights), F32),
        ),
        in_specs=[
            along(species, nodes), along(velocity.shape[0], nodes), along(species, FACES * pad),
            whole(derivatives.shape), whole(lift_operator.shape[::-1]), whole(emission_profile.shape[::-1]),
            whole(spread.shape), along(1), whole(slots.shape),
        ],
        out_specs=(along(species, nodes), whole((tile_count, species * heights))),
        scratch_shapes=[pltpu.VMEM((nodes, FACES * pad), BF16)],
        compiler_params=pltpu.CompilerParams(vmem_limit_bytes=24 * 2**20),
        name="step",
    )(
        adjoint, velocity, flux, derivatives, lift_operator.T, emission_profile.T,
        spread, element_tile.reshape(1, elements), slots,
    )

    own = tile_count // (n_group * n_sub)
    width = species * heights
    emission_grad = pl.pallas_call(
        functools.partial(sum_kernel, n_group, n_sub),
        out_shape=jax.ShapeDtypeStruct((own, width), F32),
        in_specs=[vmem],
        out_specs=vmem,
        scratch_shapes=[
            pltpu.VMEM((n_sub, n_group, own, width), BF16),
            pltpu.VMEM((n_sub, n_group, own, width), BF16),
            pltpu.VMEM((n_group, own, width), F32),
            pltpu.VMEM((n_group, own, width), F32),
            dma((n_sub,)), dma((n_sub,)), dma((n_group,)), dma((n_group,)),
        ],
        compiler_params=pltpu.CompilerParams(
            collective_id=1, has_side_effects=True, vmem_limit_bytes=16 * 2**20),
        name="sum",
    )(partial)
    return adjoint_next, emission_grad


def solution(mesh):
    both = ("group", "sub")
    placed = (
        P(None, None, both), P(None, None, both), P(None, both), P(), P(), P(),
        P(None, both), P(None, both), P(None, both), P(both), P(),
    )
    return jax.shard_map(
        functools.partial(on_device, mesh.shape["group"], mesh.shape["sub"]),
        mesh=mesh,
        in_specs=placed,
        out_specs=(P(None, None, both), P(both, None)),
        check_vma=False,
    )
```

```python
import functools

import jax
import jax.numpy as jnp
import numpy as np
from jax import lax
from jax.experimental import pallas as pl
from jax.experimental.pallas import tpu as pltpu
from jax.sharding import PartitionSpec as P

ORDER = 5
SECTION = 0.125
FACES = 6
SPAN = 256
WIDE = 512
MESH = pl.DeviceIdType.MESH
F32, BF16 = jnp.float32, jnp.bfloat16


def face_table(order):
    edge = order + 1
    a, b = np.meshgrid(np.arange(edge), np.arange(edge), indexing="ij")
    a, b = a.reshape(-1), b.reshape(-1)
    rows = []
    for axis_id in range(3):
        for level in (0, edge - 1):
            fixed = a * 0 + level
            i, j, l = [(fixed, a, b), (a, fixed, b), (a, b, fixed)][axis_id]
            rows.append((i * edge + j) * edge + l)
    return np.stack(rows).astype(np.int32)


def padded_nodes(face_nodes):
    return -(-face_nodes // 8) * 8


def select_matrix(node_count):
    table = face_table(ORDER)
    pad = padded_nodes(table.shape[1])
    out = np.zeros((FACES * pad, node_count), np.float32)
    for f in range(FACES):
        for k, n in enumerate(table[f]):
            out[f * pad + k, n] = 1
    return out


def spread_matrix(face_nodes):
    pad = padded_nodes(face_nodes)
    out = np.zeros((FACES * pad, FACES * face_nodes), np.float32)
    for f in range(FACES):
        for k in range(face_nodes):
            out[f * pad + k, f * face_nodes + k] = 1
    return out


def dot(a, b):
    return jnp.dot(a, b, preferred_element_type=F32)


def dot_nt(a, b):
    return lax.dot_general(a, b, (((1,), (1,)), ((), ())), preferred_element_type=F32)


def one_hot_rows(index, rows):
    ids = lax.broadcasted_iota(jnp.int32, (rows, index.shape[1]), 0).astype(jnp.int16)
    return jnp.where(ids == index.astype(jnp.int16), jnp.ones((), BF16), jnp.zeros((), BF16))


def columns_of(stack, position, first, count, block):
    picked = dot(stack, one_hot_rows(position & (SPAN - 1), SPAN))
    tile = position >> (SPAN.bit_length() - 1)
    out = picked[:block]
    for t in range(1, count):
        out = jnp.where(tile == first + t, picked[t * block : (t + 1) * block], out)
    return out


def flux_kernel(
    n_group, n_sub, cap,
    adjoint, speed_hbm, neighbours_hbm, sub_sends_hbm, group_sends_hbm, select_hbm, spread_hbm,
    flux,
    speed, neighbours, sub_sends, group_sends, select, spread,
    field, table, local, send_sub, recv_sub, send_group, recv_group, far_sub, flux_out,
    load_sem, flux_sem, field_sem, sub_send_sem, sub_recv_sem, group_send_sem, group_recv_sem,
):
    tiles, species = field.shape[0], field.shape[1]
    pad = select.shape[0] // FACES
    block = species * pad
    elements = tiles * SPAN
    g, q = lax.axis_index("group"), lax.axis_index("sub")
    above = (lax.rem(g + 1, n_group), q)
    below = (lax.rem(g + n_group - 1, n_group), q)

    def field_copy(i):
        cols = pl.ds(pl.multiple_of(i * SPAN, SPAN), SPAN)
        return pltpu.make_async_copy(adjoint.at[:, :, cols], field.at[i], field_sem.at[i])

    pairs = [
        (select_hbm, select), (sub_sends_hbm, sub_sends), (group_sends_hbm, group_sends),
        (neighbours_hbm, neighbours), (spread_hbm, spread), (speed_hbm, speed),
    ]
    loads = [pltpu.make_async_copy(a, b, load_sem.at[i]) for i, (a, b) in enumerate(pairs)]
    loads[0].start()
    for i in range(tiles):
        field_copy(i).start()
    for load in loads[1:]:
        load.start()

    barrier = pltpu.get_barrier_semaphore()
    peers = [(g, lax.rem(q + d, n_sub)) for d in range(1, n_sub)] + [above, below]
    for peer in peers:
        pl.semaphore_signal(barrier, inc=1, device_id=peer, device_id_type=MESH)

    loads[0].wait()

    def trace_tile(i, carry):
        for j in range(WIDE // SPAN):
            field_copy(i * (WIDE // SPAN) + j).wait()
        for j in range(WIDE // SPAN):
            tile = i * (WIDE // SPAN) + j
            parts = [dot(select[...], field[tile, s].astype(BF16)) for s in range(species)]
            rows = pl.ds(pl.multiple_of(tile * block, block), block)
            for f in range(FACES):
                one = jnp.concatenate([p[f * pad : (f + 1) * pad] for p in parts], axis=0)
                table[f, rows, :] = one.astype(BF16)
        return carry

    lax.fori_loop(0, tiles * SPAN // WIDE, trace_tile, 0)

    for load in loads[1:]:
        load.wait()
    low_half = lax.broadcasted_iota(jnp.int32, (block, 2 * cap), 1) < cap
    for axis_id in range(2):
        for c in range(n_sub * cap // WIDE):
            cols = slice(c * WIDE, (c + 1) * WIDE)
            minus, plus = [
                columns_of(table[f], sub_sends[f : f + 1, cols], 0, tiles, block)
                for f in (2 * axis_id, 2 * axis_id + 1)
            ]
            for m in range(WIDE // (2 * cap)):
                part = slice(m * 2 * cap, (m + 1) * 2 * cap)
                a, b = minus[:, part], plus[:, part]
                r = c * (WIDE // cap) + 2 * m
                send_sub[r, axis_id] = jnp.where(low_half, a, pltpu.roll(b, cap, 1)).astype(BF16)
                send_sub[r + 1, axis_id] = jnp.where(low_half, pltpu.roll(a, cap, 1), b).astype(BF16)
    pl.semaphore_wait(barrier, len(peers))
    copies = []
    for d in range(1, n_sub):
        peer = lax.rem(q + d, n_sub)
        copies.append(
            pltpu.make_async_remote_copy(
                src_ref=send_sub.at[peer], dst_ref=recv_sub.at[q],
                send_sem=sub_send_sem.at[d], recv_sem=sub_recv_sem.at[d],
                device_id=(g, peer), device_id_type=MESH,
            )
        )
        copies[-1].start()
    span_group = send_group.shape[2]
    for k, target in ((0, below), (1, above)):
        for c in range(span_group // SPAN):
            cols = slice(c * SPAN, (c + 1) * SPAN)
            got = columns_of(table[4 + k], group_sends[k : k + 1, cols], 0, tiles, block)
            send_group[k, :, cols] = got.astype(BF16)
        copies.append(
            pltpu.make_async_remote_copy(
                src_ref=send_group.at[k], dst_ref=recv_group.at[k],
                send_sem=group_send_sem.at[k], recv_sem=group_recv_sem.at[k],
                device_id=target, device_id_type=MESH,
            )
        )
        copies[-1].start()
    recv_sub[q] = jnp.zeros(recv_sub.shape[1:], BF16)

    def local_tile(i, carry):
        cols = pl.ds(pl.multiple_of(i * WIDE, WIDE), WIDE)
        for f in range(FACES):
            got = columns_of(table[f ^ 1], neighbours[f : f + 1, cols], 0, tiles, block)
            local[f, :, cols] = got.astype(BF16)
        return carry

    lax.fori_loop(0, elements // WIDE, local_tile, 0)

    for copy in copies:
        copy.wait()
    far_tiles = n_sub * cap // SPAN
    for t in range(4):
        for r in range(0, n_sub, 2):
            a = recv_sub[r, t // 2].astype(F32)
            b = recv_sub[r + 1, t // 2].astype(F32)
            if t % 2 == 0:
                both = jnp.where(low_half, a, pltpu.roll(b, cap, 1))
            else:
                both = jnp.where(low_half, pltpu.roll(a, cap, 1), b)
            lane = r * cap
            far_sub[t, (lane // SPAN) * block : (lane // SPAN + 1) * block,
                    lane % SPAN : lane % SPAN + 2 * cap] = both.astype(BF16)

    def flux_copy(i):
        cols = pl.ds(pl.multiple_of(i * WIDE, WIDE), WIDE)
        return pltpu.make_async_copy(flux_out.at[i], flux.at[:, :, cols], flux_sem.at[i])

    def flux_tile(i, carry):
        cols = pl.ds(pl.multiple_of(i * WIDE, WIDE), WIDE)
        inside = WIDE // SPAN
        upwind = jnp.maximum(dot(spread[...], speed[:, cols]), 0.0)
        parts = []
        for f in range(FACES):
            t = f ^ 1
            position = neighbours[f : f + 1, cols]
            if t < 4:
                far = columns_of(far_sub[t], position, tiles, far_tiles, block)
            else:
                stack = jnp.concatenate([
                    recv_group[t - 4, :, c * SPAN : (c + 1) * SPAN]
                    for c in range(span_group // SPAN)
                ], axis=0)
                far = columns_of(stack, position, tiles + far_tiles, span_group // SPAN, block)
            outside = jnp.where(position >= elements, far, local[f, :, cols].astype(F32))
            wind = jnp.concatenate([upwind[f * pad : (f + 1) * pad]] * species, axis=0)
            here = jnp.concatenate([
                table[f, pl.ds(pl.multiple_of((i * inside + j) * block, block), block), :]
                for j in range(inside)
            ], axis=1)
            parts.append(wind * (outside - here.astype(F32)))
        for s in range(species):
            one = jnp.concatenate([p[s * pad : (s + 1) * pad] for p in parts], axis=0)
            flux_out[i, s] = one.astype(BF16)
        flux_copy(i).start()
        return carry

    lax.fori_loop(0, elements // WIDE, flux_tile, 0)
    for i in range(elements // WIDE):
        flux_copy(i).wait()


def step_kernel(
    adjoint, velocity, flux, derivatives, lift, profile, spread, element_tile, tile_slot,
    adjoint_next, partial, lift_wide,
):
    species, nodes, span = adjoint.shape
    tile_rows = partial.shape[0]

    @pl.when(pl.program_id(0) == 0)
    def _():
        lift_wide[...] = dot(spread[...], lift[...]).T.astype(BF16)
        partial[...] = jnp.zeros_like(partial)

    tile = element_tile[...]
    width = tile_slot.shape[1]
    slots = tile_slot[...]
    high = dot((slots >> 8).astype(F32).astype(BF16), one_hot_rows(lax.rem(tile, width), width))
    low = dot((slots & 255).astype(F32).astype(BF16), one_hot_rows(lax.rem(tile, width), width))
    picked = (high * 256.0 + low)
    which = lax.broadcasted_iota(jnp.int32, picked.shape, 0) == lax.div(tile, width)
    row = jnp.sum(jnp.where(which, picked, 0.0), axis=0, keepdims=True).astype(jnp.int32)

    contrib = []
    wind = [velocity[d].astype(F32) for d in range(3)]
    for s in range(species):
        field = adjoint[s]
        grads = dot(derivatives[...], field.astype(BF16))
        total = dot(lift_wide[...], flux[s])
        for d in range(3):
            total += wind[d] * grads[d * nodes : (d + 1) * nodes]
        result = field + SECTION * total
        adjoint_next[s] = result
        contrib.append(dot(profile[...], result.astype(BF16)))
    terms = jnp.concatenate(contrib, axis=0)
    first = terms.astype(BF16)
    second = (terms - first.astype(F32)).astype(BF16)
    both = jnp.concatenate([first, second], axis=0)
    sums = dot_nt(one_hot_rows(row, tile_rows), both)
    half = terms.shape[0]
    partial[...] += sums[:, :half] + sums[:, half:]


def sum_kernel(
    n_group, n_sub,
    partial_hbm, out,
    partial, send, recv, mid, recv_mid,
    load_sem, send_sem, recv_sem, mid_send_sem, mid_recv_sem,
):
    load = pltpu.make_async_copy(partial_hbm, partial, load_sem)
    load.start()
    own = out.shape[0]
    g, q = lax.axis_index("group"), lax.axis_index("sub")
    barrier = pltpu.get_barrier_semaphore()
    peers = [(g, lax.rem(q + d, n_sub)) for d in range(1, n_sub)]
    peers += [(lax.rem(g + d, n_group), q) for d in range(1, n_group)]
    for peer in peers:
        pl.semaphore_signal(barrier, inc=1, device_id=peer, device_id_type=MESH)

    def rows_of(group, sub):
        return pl.ds(pl.multiple_of((group * n_sub + sub) * own, own), own)

    load.wait()
    for d in range(1, n_sub):
        for k in range(n_group):
            send[d, k] = partial[rows_of(k, lax.rem(q + d, n_sub)), :].astype(BF16)
    pl.semaphore_wait(barrier, len(peers))
    copies = []
    for d in range(1, n_sub):
        copies.append(
            pltpu.make_async_remote_copy(
                src_ref=send.at[d], dst_ref=recv.at[d],
                send_sem=send_sem.at[d], recv_sem=recv_sem.at[d],
                device_id=(g, lax.rem(q + d, n_sub)), device_id_type=MESH,
            )
        )
        copies[-1].start()
    for k in range(n_group):
        mid[k] = partial[rows_of(k, q), :]
    for copy in copies:
        copy.wait()
    for k in range(n_group):
        total = mid[k]
        for d in range(1, n_sub):
            total += recv[d, k].astype(F32)
        mid[k] = total
    copies = []
    for d in range(1, n_group):
        other = lax.rem(g + d, n_group)
        copies.append(
            pltpu.make_async_remote_copy(
                src_ref=mid.at[other], dst_ref=recv_mid.at[d],
                send_sem=mid_send_sem.at[d], recv_sem=mid_recv_sem.at[d],
                device_id=(other, q), device_id_type=MESH,
            )
        )
        copies[-1].start()
    for copy in copies:
        copy.wait()
    total = mid[g]
    for d in range(1, n_group):
        total += recv_mid[d]
    out[...] = total


def on_device(
    n_group, n_sub,
    adjoint, velocity, face_speed, derivatives, lift_operator, emission_profile,
    neighbours, sub_sends, group_sends, element_tile, tile_slot,
):
    species, nodes, elements = adjoint.shape
    face_nodes = face_speed.shape[0] // FACES
    pad = padded_nodes(face_nodes)
    block = species * pad
    tiles = elements // SPAN
    cap = sub_sends.shape[1] // n_sub
    span_group = group_sends.shape[1]
    assert elements % WIDE == 0 and n_sub * cap % WIDE == 0 and SPAN % (2 * cap) == 0 and 2 * cap == 128
    assert (n_sub * cap) % SPAN == 0 and span_group % SPAN == 0
    select = jnp.asarray(select_matrix(nodes), BF16)
    spread = jnp.asarray(spread_matrix(face_nodes), BF16)
    vmem = pl.BlockSpec(memory_space=pltpu.VMEM)
    dma = pltpu.SemaphoreType.DMA
    far_tiles = n_sub * cap // SPAN

    flux = pl.pallas_call(
        functools.partial(flux_kernel, n_group, n_sub, cap),
        out_shape=jax.ShapeDtypeStruct((species, FACES * pad, elements), BF16),
        in_specs=[pl.BlockSpec(memory_space=pl.ANY)] * 7,
        out_specs=pl.BlockSpec(memory_space=pl.ANY),
        scratch_shapes=[
            *[
                pltpu.VMEM(a.shape, a.dtype)
                for a in (face_speed, neighbours, sub_sends, group_sends, select, spread)
            ],
            pltpu.VMEM((tiles, species, nodes, SPAN), F32),
            pltpu.VMEM((FACES, tiles * block, SPAN), BF16),
            pltpu.VMEM((FACES, block, elements), BF16),
            pltpu.VMEM((n_sub, 2, block, 2 * cap), BF16),
            pltpu.VMEM((n_sub, 2, block, 2 * cap), BF16),
            pltpu.VMEM((2, block, span_group), BF16),
            pltpu.VMEM((2, block, span_group), BF16),
            pltpu.VMEM((4, far_tiles * block, SPAN), BF16),
            pltpu.VMEM((elements // WIDE, species, FACES * pad, WIDE), BF16),
            dma((6,)), dma((elements // WIDE,)),
            dma((tiles,)), dma((n_sub,)), dma((n_sub,)), dma((2,)), dma((2,)),
        ],
        compiler_params=pltpu.CompilerParams(
            collective_id=0, has_side_effects=True, vmem_limit_bytes=56 * 2**20),
        name="flux",
    )(adjoint, face_speed, neighbours, sub_sends, group_sends, select, spread)

    tile_count = tile_slot.shape[0]
    heights = emission_profile.shape[1]
    whole = lambda shape: pl.BlockSpec(shape, lambda i: (0,) * len(shape))
    along = lambda *lead: pl.BlockSpec(lead + (WIDE,), lambda i: (0,) * len(lead) + (i,))
    slots = tile_slot.reshape(tile_count // 128, 128)
    adjoint_next, partial = pl.pallas_call(
        step_kernel,
        grid=(elements // WIDE,),
        out_shape=(
            jax.ShapeDtypeStruct(adjoint.shape, F32),
            jax.ShapeDtypeStruct((tile_count, species * heights), F32),
        ),
        in_specs=[
            along(species, nodes), along(velocity.shape[0], nodes), along(species, FACES * pad),
            whole(derivatives.shape), whole(lift_operator.shape[::-1]), whole(emission_profile.shape[::-1]),
            whole(spread.shape), along(1), whole(slots.shape),
        ],
        out_specs=(along(species, nodes), whole((tile_count, species * heights))),
        scratch_shapes=[pltpu.VMEM((nodes, FACES * pad), BF16)],
        compiler_params=pltpu.CompilerParams(vmem_limit_bytes=56 * 2**20),
        name="step",
    )(
        adjoint, velocity, flux, derivatives, lift_operator.T, emission_profile.T,
        spread, element_tile.reshape(1, elements), slots,
    )

    own = tile_count // (n_group * n_sub)
    width = species * heights
    emission_grad = pl.pallas_call(
        functools.partial(sum_kernel, n_group, n_sub),
        out_shape=jax.ShapeDtypeStruct((own, width), F32),
        in_specs=[pl.BlockSpec(memory_space=pl.ANY)],
        out_specs=vmem,
        scratch_shapes=[
            pltpu.VMEM((tile_count, width), F32),
            pltpu.VMEM((n_sub, n_group, own, width), BF16),
            pltpu.VMEM((n_sub, n_group, own, width), BF16),
            pltpu.VMEM((n_group, own, width), F32),
            pltpu.VMEM((n_group, own, width), F32),
            dma, dma((n_sub,)), dma((n_sub,)), dma((n_group,)), dma((n_group,)),
        ],
        compiler_params=pltpu.CompilerParams(
            collective_id=1, has_side_effects=True, vmem_limit_bytes=56 * 2**20),
        name="sum",
    )(partial)
    return adjoint_next, emission_grad


def solution(mesh):
    both = ("group", "sub")
    placed = (
        P(None, None, both), P(None, None, both), P(None, both), P(), P(), P(),
        P(None, both), P(None, both), P(None, both), P(both), P(),
    )
    return jax.shard_map(
        functools.partial(on_device, mesh.shape["group"], mesh.shape["sub"]),
        mesh=mesh,
        in_specs=placed,
        out_specs=(P(None, None, both), P(both, None)),
        check_vma=False,
    )
```
